256 devices in a mesh: seq: 32 (over z, y), head: 8 (over x, core).
Axes of the slice: x: 4, y: 4, z: 8, core: 2. Of those that a mesh axis runs over, the one named last changes fastest.
Arguments:
- queries: bfloat16 [16384, 7168], P('seq', 'head'), may hold values from -140 to 140
- keys: bfloat16 [16384, 7168], P('seq', 'head'), may hold values from -7 to 7
- values: bfloat16 [16384, 7168], P('seq', 'head'), may hold values from -6 to 6
- out_grad: bfloat16 [16384, 7168], P(('seq', 'head')), may hold values from -6 to 6
- selection: int32 [512, 3], replicated, may hold values from 0 to 31, as said below
Outputs:
- query_grad: bfloat16 [16384, 7168], P('seq', 'head')
- key_grad: bfloat16 [16384, 7168], P('seq', 'head')
- value_grad: bfloat16 [16384, 7168], P('seq', 'head')
The draws below stay inside these ranges and needn't reach their ends.
Inputs may be any that keep to these rules, and one draw needn't show every extreme that they name: `selection`: row c lists the key blocks selected by query stretch c, whose own block is c // 16. An entry equal to the own block selects nothing; every other entry names an earlier block, and the entries of a row that select something are distinct. The 16 stretches of one own block together name each earlier block at most once, and name block 0 exactly once when their own block is not 0.
All inputs are finite; a program needn't handle non-finite values.
Results may differ from the reference program's by a relative error of at most 0.0065.
Values may be sent and summed in bfloat16 or wider, within the bound.
A program may use at most 128 MiB of HBM per device.

```python
import math
import jax
import jax.numpy as jnp
from jax import lax

HEADS = 56
HD = 128
BLOCK = 512
QCHUNK = 32
SEQ = 16384
STRETCHES = 512


def key_base(key):
    return jnp.clip(jax.random.normal(key, (SEQ, HEADS * HD), jnp.float32), -6.0, 6.0)


def draw_keys(key, part):
    base = key_base(key)
    return base.astype(jnp.bfloat16)


def draw_queries(key, part):
    key = jax.random.fold_in(key, 1)
    fresh = jnp.clip(jax.random.normal(key, (SEQ, HEADS * HD), jnp.float32), -6.0, 6.0)
    return fresh.astype(jnp.bfloat16)


def draw_selection(key, part):
    key = jax.random.fold_in(key, 7)
    blocks = STRETCHES * QCHUNK // BLOCK
    stretch_count = BLOCK // QCHUNK

    def one_block(device):
        subkey = jax.random.fold_in(key, device)
        slots = jax.random.permutation(jax.random.fold_in(subkey, 1), 3 * stretch_count)[:blocks].astype(jnp.int32)
        keeps = jax.random.randint(jax.random.fold_in(subkey, 2), (blocks,), 0, 4) > 0
        block_ids = jnp.arange(blocks, dtype=jnp.int32)
        chosen = (block_ids < device) & (keeps | (block_ids == 0))
        table = jnp.full((3 * stretch_count,), device, jnp.int32).at[slots].set(jnp.where(chosen, block_ids, device))
        return table.reshape(stretch_count, 3)
    return jax.vmap(one_block)(jnp.arange(blocks, dtype=jnp.int32)).reshape(STRETCHES, 3).astype(jnp.int32)


def block_scale(own_key, extent, split, low, top_value):
    factor_of, own = 1.0, jax.random.fold_in(own_key, 6)
    for position, parts in split:
        draws = jnp.exp(jax.random.uniform(jax.random.fold_in(own, position), (parts,), jnp.float32, low / len(split), top_value / len(split)))
        factor_of = factor_of * jnp.repeat(draws, extent[position] // parts).reshape([-1 if axis == position else 1 for axis in range(len(extent))])
    return factor_of


def gaussian(rng, shape, width, reach, pieces=(), kind=jnp.bfloat16):
    factor_of = block_scale(rng, shape, pieces, -0.22, 0.18) if pieces else 1.0
    values = jax.random.normal(rng, shape, jnp.float32) * width * factor_of
    return jnp.minimum(jnp.maximum(values, -reach), reach).astype(kind)


def setup_inputs(seed: int = 0) -> dict:
    splits = jax.random.split(jax.random.key(seed), 6)
    queries = draw_queries(jax.random.fold_in(splits[5], 71), 0)
    keys = draw_keys(jax.random.fold_in(splits[5], 71), 0)
    values = gaussian(splits[2], (SEQ, HEADS * HD), 1.0, 6.0, ((0, 32), (1, 8)))
    out_grad = gaussian(splits[3], (SEQ, HEADS * HD), 1.0, 6.0, ((0, 256),))
    selection = draw_selection(jax.random.fold_in(splits[5], 71), 0)
    return dict(queries=queries, keys=keys, values=values, out_grad=out_grad, selection=selection)


def reference(queries, keys, values, out_grad, selection):
    scale = 1.0 / math.sqrt(HD)
    stretch_count = BLOCK // QCHUNK
    features = HEADS * HD
    span = 4 * BLOCK

    def stretch_step(buffers, stretch_index):
        key_acc, value_acc = buffers
        block_index = (stretch_index // stretch_count).astype(jnp.int32)
        lists = selection[stretch_index].astype(jnp.int32)
        block_ids = jnp.concatenate([block_index[None], lists]).astype(jnp.int32)
        live = jnp.concatenate([jnp.array([True]), lists != block_index])
        key_rows = (block_ids[:, None] * BLOCK + jnp.arange(BLOCK, dtype=jnp.int32)[None, :]).reshape(-1).astype(jnp.int32)
        key_part = keys[key_rows].astype(jnp.float32).reshape(span, HEADS, HD)
        value_part = values[key_rows].astype(jnp.float32).reshape(span, HEADS, HD)
        start = (stretch_index * QCHUNK).astype(jnp.int32)
        query_part = lax.dynamic_slice_in_dim(queries, start, QCHUNK, 0).astype(jnp.float32).reshape(QCHUNK, HEADS, HD)
        grad_part = lax.dynamic_slice_in_dim(out_grad, start, QCHUNK, 0).astype(jnp.float32).reshape(QCHUNK, HEADS, HD)
        scores = jnp.einsum('qhd,khd->hqk', query_part, key_part) * scale
        query_pos = start + jnp.arange(QCHUNK, dtype=jnp.int32)
        own_part = jnp.arange(span, dtype=jnp.int32) < BLOCK
        allowed = jnp.where(own_part[None, :], key_rows[None, :] <= query_pos[:, None], jnp.repeat(live, BLOCK)[None, :])
        scores = jnp.where(allowed[None], scores, -jnp.inf)
        row_max = lax.optimization_barrier(jnp.max(scores, axis=2))
        log_total = row_max + jnp.log(lax.optimization_barrier(jnp.sum(jnp.exp(scores - row_max[:, :, None]), axis=2)))
        prob = jnp.exp(scores - log_total[:, :, None])
        grad_prob = jnp.einsum('qhd,khd->hqk', grad_part, value_part)
        row_delta = lax.optimization_barrier(jnp.sum(prob * grad_prob, axis=2))
        grad_score = lax.optimization_barrier((prob * (grad_prob - row_delta[:, :, None]) * scale).astype(jnp.bfloat16)).astype(jnp.float32)
        prob_half = lax.optimization_barrier(prob.astype(jnp.bfloat16)).astype(jnp.float32)
        grad_query = jnp.einsum('hqk,khd->qhd', grad_score, key_part).reshape(QCHUNK, features).astype(jnp.bfloat16)
        key_term = jnp.einsum('hqk,qhd->khd', grad_score, query_part).reshape(span, features)
        value_term = jnp.einsum('hqk,qhd->khd', prob_half, grad_part).reshape(span, features)
        return ((key_acc.at[key_rows].add(key_term), value_acc.at[key_rows].add(value_term)), grad_query)
    empty = jnp.zeros((SEQ, features), jnp.float32)
    (key_acc, value_acc), query_rows = lax.scan(stretch_step, (empty, empty), jnp.arange(STRETCHES, dtype=jnp.int32))
    return (query_rows.reshape(SEQ, features), key_acc.astype(jnp.bfloat16), value_acc.astype(jnp.bfloat16))
```

```python
import functools
import math

import jax
import jax.numpy as jnp
from jax import lax
from jax.experimental import pallas as pl
from jax.experimental.pallas import tpu as pltpu
from jax.sharding import PartitionSpec as P

HD = 128
QCHUNK = 32
TILE_SLOTS = 8
TILE = TILE_SLOTS * QCHUNK
GROUP = 128 // QCHUNK
PIECES = 4
SCALE = 1.0 / math.sqrt(HD)
EXPO = SCALE * math.log2(math.e)
NEG = -1e30
BIG = 1e30
NT_DIMS = (((1,), (1,)), ((), ()))
MESH = pl.DeviceIdType.MESH


def head_chunks(head_count):
    edges = list(range(0, head_count, 2)) + [head_count]
    return tuple(zip(edges[:-1], edges[1:]))


def dot(lhs, rhs):
    return jnp.dot(lhs, rhs, preferred_element_type=jnp.float32)


def dot_nt(lhs, rhs):
    return lax.dot_general(lhs, rhs, NT_DIMS, preferred_element_type=jnp.float32)


def score_columns(key_tile, query_tile, diagonal):
    scores = dot_nt(key_tile, query_tile)
    if diagonal is not None:
        rows = lax.broadcasted_iota(jnp.int32, scores.shape, 0)
        cols = lax.broadcasted_iota(jnp.int32, scores.shape, 1)
        scores = jnp.where(rows <= cols + diagonal, scores, NEG)
    return scores


def stats_tile(key_tile, value_tile, query_tile, grad_tile, diagonal, weight_ref, prob_ref, top_ref):
    scores = score_columns(key_tile, query_tile, diagonal)
    grad_prob = dot_nt(value_tile, grad_tile)
    prob_ref[...] = grad_prob
    rows = scores.shape[0] // PIECES
    tops, totals, inners = [], [], []
    for piece in range(PIECES):
        span = slice(piece * rows, piece * rows + rows)
        top = jnp.max(scores[span], axis=0, keepdims=True)
        weights = jnp.exp2((scores[span] - top) * EXPO)
        weight_ref[span] = weights
        top_ref[piece : piece + 1] = top
        tops.append(top)
        totals.append(jnp.sum(weights, axis=0, keepdims=True))
        inners.append(jnp.sum(weights * grad_prob[span], axis=0, keepdims=True))
    best = functools.reduce(jnp.maximum, tops)
    factors = [jnp.exp2((top - best) * EXPO) for top in tops]
    total = sum(factor * part for factor, part in zip(factors, totals))
    inner = sum(factor * part for factor, part in zip(factors, inners))
    return best, total, inner


def grads_tile(key_t, query_tile, grad_tile, log_row, delta_row, weight_ref, prob_ref, top_ref):
    rows = weight_ref.shape[0] // PIECES
    probs, scores = [], []
    for piece in range(PIECES):
        span = slice(piece * rows, piece * rows + rows)
        prob = weight_ref[span] * jnp.exp2((top_ref[piece : piece + 1] - log_row) * EXPO)
        probs.append(prob.astype(jnp.bfloat16))
        scores.append((prob * (prob_ref[span] - delta_row)).astype(jnp.bfloat16))
    prob_half = jnp.concatenate(probs, axis=0)
    grad_score = jnp.concatenate(scores, axis=0)
    grad_key = dot(grad_score, query_tile)
    grad_value = dot(prob_half, grad_tile)
    grad_query = dot(key_t, grad_score).T
    return grad_query, grad_key, grad_value


def quarter_swap(parts, target):
    lane = lax.broadcasted_iota(jnp.int32, parts[0].shape, 1) // QCHUNK
    out = jnp.zeros(parts[0].shape, jnp.float32)
    for source, part in enumerate(parts):
        shift = ((source - target) * QCHUNK) % 128
        moved = pltpu.roll(part, shift, 1) if shift else part
        out = jnp.where(lane == source, moved, out)
    return out


def kernel(n, nh, heads, chunks, *refs):
    refs = list(refs)
    sent_stretch, sent_used, own_pick, own_live = refs[:4]
    q_ref, k_ref, v_ref, g_ref = refs[4:8]
    dq_ref, dk_ref, dv_ref = refs[8:11]
    g_own, k_t, dk_acc, dv_acc, dq_own = refs[11:16]
    stat_far, stat_own, own_rows, far_rows, logs_own, log_far, delta_far, log_head, delta_head = refs[16:25]
    head_send, head_recv = refs[25:27]
    far_kept, high_kept, low_kept = refs[27:30], refs[30:33], refs[33:36]
    rest = refs[36:]
    buffers = []
    for _ in chunks:
        buffers.append(rest[:20])
        rest = rest[20:]

    me = lax.axis_index("seq")
    hx = lax.axis_index("head")
    stretches = q_ref.shape[0]
    block = stretches * QCHUNK
    feats = heads * HD
    piece = stretches // nh
    tiles = n // TILE_SLOTS
    first_tile = (me + 1) // TILE_SLOTS

    def head_cols(head):
        return pl.ds(pl.multiple_of(head * HD, HD), HD)

    barrier = pltpu.get_barrier_semaphore()

    def greet_seq(step, carry):
        peer = lax.rem(me + step, n)
        pl.semaphore_signal(barrier, inc=1, device_id=(peer, hx), device_id_type=MESH)
        return carry

    def greet_head(step, carry):
        peer = lax.rem(hx + step, nh)
        pl.semaphore_signal(barrier, inc=1, device_id=(me, peer), device_id_type=MESH)
        return carry

    lax.fori_loop(1, n, greet_seq, 0)
    lax.fori_loop(1, nh, greet_head, 0)
    pl.semaphore_wait(barrier, n - 1 + nh - 1)

    def head_copy(peer, slot):
        return pltpu.make_async_remote_copy(
            src_ref=g_ref.at[:, :, pl.ds(pl.multiple_of(peer * feats, HD), feats)],
            dst_ref=g_own.at[pl.ds(slot * piece, piece)],
            send_sem=head_send.at[peer],
            recv_sem=head_recv.at[slot],
            device_id=(me, peer),
            device_id_type=MESH,
        )

    def start_head(step, carry):
        head_copy(lax.rem(hx + step, nh), hx).start()
        return carry

    lax.fori_loop(1, nh, start_head, 0)

    def pair_copy(src, dst, send, recv, peer, slot):
        return pltpu.make_async_remote_copy(
            src_ref=src.at[peer],
            dst_ref=dst.at[slot],
            send_sem=send.at[peer],
            recv_sem=recv.at[slot],
            device_id=(peer, hx),
            device_id_type=MESH,
        )

    def mixed(i):
        return lax.rem(i * 13, n - 1) + 1

    def each_near(body):
        def step(i, carry):
            shift = mixed(i)

            @pl.when(shift <= me)
            def _():
                body(me - shift)

            return carry

        lax.fori_loop(0, n - 1, step, 0)

    def each_far(body):
        def step(i, carry):
            shift = mixed(i)

            @pl.when(me + shift < n)
            def _():
                body(me + shift)

            return carry

        lax.fori_loop(0, n - 1, step, 0)

    def send_rows(source, src, dst, send, recv, start, stop):
        def body(peer):
            row = sent_stretch[peer]
            for head in range(start, stop):
                src[peer, head - start] = source[row, :, head * HD : head * HD + HD]
            pair_copy(src, dst, send, recv, peer, me).start()

        each_near(body)

    def wait_far(src, dst, send, recv):
        def step(peer, carry):
            pair_copy(src, dst, send, recv, peer, peer).wait_recv()
            return carry

        lax.fori_loop(me + 1, n, step, 0)

    def wait_near(src, dst, send, recv):
        def step(peer, carry):
            pair_copy(src, dst, send, recv, peer, peer).wait_recv()
            return carry

        lax.fori_loop(0, me, step, 0)

    def sent_down(src, dst, send, recv):
        def step(peer, carry):
            pair_copy(src, dst, send, recv, peer, me).wait_send()
            return carry

        lax.fori_loop(0, me, step, 0)

    def start_up(src, dst, send, recv):
        each_far(lambda peer: pair_copy(src, dst, send, recv, peer, me).start())

    def sent_up(src, dst, send, recv):
        def step(peer, carry):
            pair_copy(src, dst, send, recv, peer, me).wait_send()
            return carry

        lax.fori_loop(me + 1, n, step, 0)

    groups = []
    for held in buffers:
        groups.append(tuple(tuple(held[4 * i : 4 * i + 4]) for i in range(5)))

    for index in range(2):
        send_rows(q_ref, *groups[index][0], *chunks[index])

    def clear(slot, carry):
        for rows, grads, stats, logs, parts in groups:
            rows[1][slot] = jnp.zeros(rows[1].shape[1:], jnp.bfloat16)
            grads[1][slot] = jnp.zeros(grads[1].shape[1:], jnp.bfloat16)
            logs[1][slot, 0:1] = jnp.full((1, 128), BIG, jnp.float32)
            logs[1][slot, 1:2] = jnp.zeros((1, 128), jnp.float32)
        return carry

    lax.fori_loop(0, me + 1, clear, 0)

    def turn(head, carry):
        k_t[head] = k_ref[:, head_cols(head)].T
        return carry

    lax.fori_loop(0, heads, turn, 0)

    g_own[pl.ds(hx * piece, piece)] = g_ref[:, :, pl.ds(pl.multiple_of(hx * feats, HD), feats)]

    def wait_head(step, carry):
        peer = lax.rem(hx + step, nh)
        head_copy(peer, peer).wait_recv()
        return carry

    lax.fori_loop(1, nh, wait_head, 0)
    send_rows(g_own, *groups[0][1], *chunks[0])

    half = block // 2
    middle = stretches // 2

    def own_tile(source, upper, cols):
        places = slice(middle, stretches) if upper else slice(0, middle)
        return source[places, :, cols].reshape(half, HD)

    def pad_stats(top, total, inner):
        return jnp.concatenate([top, total, inner, jnp.zeros((5, top.shape[1]), jnp.float32)], axis=0)

    def own_stats(head, carry):
        cols = head_cols(head)
        stat_own[head, :, 0:half] = pad_stats(
            *stats_tile(
                k_ref[0:half, cols], v_ref[0:half, cols], own_tile(q_ref, False, cols), own_tile(g_own, False, cols), 0,
                *(kept.at[head] for kept in low_kept),
            )
        )
        stat_own[head, :, half:block] = pad_stats(
            *stats_tile(
                k_ref[:, cols], v_ref[:, cols], own_tile(q_ref, True, cols), own_tile(g_own, True, cols), half,
                *(kept.at[head] for kept in high_kept),
            )
        )
        return carry

    lax.fori_loop(0, heads, own_stats, 0)

    def chunk_stats(chunk):
        (start, stop), (rows, grads, stats, logs, parts) = chunks[chunk], groups[chunk]
        count = stop - start
        wait_far(*rows)
        wait_far(*grads)

        def far_stats(tile, carry):
            slots = pl.ds(pl.multiple_of(tile * TILE_SLOTS, TILE_SLOTS), TILE_SLOTS)
            for local in range(count):
                cols = pl.ds((local + start) * HD, HD)
                query_tile = rows[1][slots, local].reshape(TILE, HD)
                grad_tile = grads[1][slots, local].reshape(TILE, HD)
                stat_far[local, :, pl.ds(pl.multiple_of(tile * TILE, TILE), TILE)] = pad_stats(
                    *stats_tile(
                        k_ref[:, cols], v_ref[:, cols], query_tile, grad_tile, None,
                        *(kept.at[chunk % 2, local, tile] for kept in far_kept),
                    )
                )
            return carry

        lax.fori_loop(first_tile, tiles, far_stats, 0)

        def far_swap(group, carry):
            lanes = pl.ds(pl.multiple_of(group * 128, 128), 128)
            held = [stat_far[local, :, lanes] for local in range(count)]
            for slot in range(GROUP):
                stats[0][group * GROUP + slot] = quarter_swap(held, slot)
            return carry

        lax.fori_loop(first_tile * (TILE // 128), n // GROUP, far_swap, 0)
        start_up(*stats)

    def chunk_logs(chunk):
        (start, stop), (rows, grads, stats, logs, parts) = chunks[chunk], groups[chunk]
        count = stop - start
        for group in range(stretches // GROUP):
            held = [stat_own[start + local, :, group * 128 : group * 128 + 128] for local in range(count)]
            for slot in range(GROUP):
                swapped = quarter_swap(held, slot)
                row = group * GROUP + slot
                for kind in range(3):
                    own_rows[kind, row : row + 1] = swapped[kind : kind + 1]

        wait_near(*stats)
        fill = jnp.where(lax.broadcasted_iota(jnp.int32, (8, 128), 0) == 0, NEG, 0.0)
        for row in range(stretches):
            for pick in range(3):
                live = own_live[row * 3 + pick]
                found = jnp.where(jnp.full((8, 128), live, jnp.int32) > 0, stats[1][own_pick[row * 3 + pick]], fill)
                for kind in range(3):
                    far_rows[pick, kind, row : row + 1] = found[kind : kind + 1]
        best = own_rows[0]
        for pick in range(3):
            best = jnp.maximum(best, far_rows[pick, 0])
        weight = jnp.exp2((own_rows[0] - best) * EXPO)
        total = own_rows[1] * weight
        inner = own_rows[2] * weight
        for pick in range(3):
            weight = jnp.exp2((far_rows[pick, 0] - best) * EXPO)
            total += far_rows[pick, 1] * weight
            inner += far_rows[pick, 2] * weight
        log_total = best + (jnp.log(total) - math.log(SCALE)) * (1.0 / SCALE)
        delta = inner / total
        for row in range(stretches):
            logs_own[row, 0:1] = log_total[row : row + 1]
            logs_own[row, 1:2] = delta[row : row + 1]

        def send_logs(peer):
            row = sent_stretch[peer]
            used = jnp.full((1, 128), sent_used[peer], jnp.int32) > 0
            logs[0][peer, 0:1] = jnp.where(used, logs_own[row, 0:1], BIG)
            logs[0][peer, 1:2] = jnp.where(used, logs_own[row, 1:2], 0.0)
            pair_copy(*logs, peer, me).start()

        each_near(send_logs)

        for group in range(stretches // GROUP):
            for kind, kept in ((0, log_head), (1, delta_head)):
                lines = [
                    jnp.broadcast_to(logs_own[group * GROUP + slot, kind : kind + 1], (8, 128))
                    for slot in range(GROUP)
                ]
                for local in range(count):
                    kept[local, :, group * 128 : group * 128 + 128] = quarter_swap(lines, local)

    def chunk_own(chunk):
        (start, stop), (rows, grads, stats, logs, parts) = chunks[chunk], groups[chunk]
        count = stop - start
        def own_grads(local, carry):
            head = local + start
            cols = head_cols(head)
            grad_query, grad_key, grad_value = grads_tile(
                k_t[head], own_tile(q_ref, True, cols), own_tile(g_own, True, cols),
                log_head[local, 0:1, half:block], delta_head[local, 0:1, half:block],
                *(kept.at[head] for kept in high_kept),
            )
            dq_own[head, half:block] = grad_query
            dk_acc[head] = grad_key
            dv_acc[head] = grad_value
            grad_query, grad_key, grad_value = grads_tile(
                k_t[head, :, 0:half], own_tile(q_ref, False, cols), own_tile(g_own, False, cols),
                log_head[local, 0:1, 0:half], delta_head[local, 0:1, 0:half],
                *(kept.at[head] for kept in low_kept),
            )
            dq_own[head, 0:half] = grad_query
            dk_acc[head, 0:half] += grad_key
            dv_acc[head, 0:half] += grad_value
            return carry

        lax.fori_loop(0, count, own_grads, 0)

    def chunk_far(chunk):
        (start, stop), (rows, grads, stats, logs, parts) = chunks[chunk], groups[chunk]
        count = stop - start
        wait_far(*logs)

        def far_logs(group, carry):
            lanes = pl.ds(pl.multiple_of(group * 128, 128), 128)
            for kind, kept in ((0, log_far), (1, delta_far)):
                lines = [
                    jnp.broadcast_to(logs[1][group * GROUP + slot, kind : kind + 1], (8, 128)) for slot in range(GROUP)
                ]
                for local in range(count):
                    kept[local, :, lanes] = quarter_swap(lines, local)
            return carry

        lax.fori_loop(first_tile * (TILE // 128), n // GROUP, far_logs, 0)

        def far_grads(tile, carry):
            slots = pl.ds(pl.multiple_of(tile * TILE_SLOTS, TILE_SLOTS), TILE_SLOTS)
            lanes = pl.ds(pl.multiple_of(tile * TILE, TILE), TILE)
            for local in range(count):
                head = local + start
                query_tile = rows[1][slots, local].reshape(TILE, HD)
                grad_tile = grads[1][slots, local].reshape(TILE, HD)
                grad_query, grad_key, grad_value = grads_tile(
                    k_t[head], query_tile, grad_tile, log_far[local, 0:1, lanes], delta_far[local, 0:1, lanes],
                    *(kept.at[chunk % 2, local, tile] for kept in far_kept),
                )
                parts[0][slots, local] = grad_query.astype(jnp.bfloat16).reshape(TILE_SLOTS, QCHUNK, HD)
                dk_acc[head] += grad_key
                dv_acc[head] += grad_value
            return carry

        lax.fori_loop(first_tile, tiles, far_grads, 0)
        start_up(*parts)

    last = len(chunks)
    for chunk in range(last):
        chunk_stats(chunk)
        if chunk + 1 < last:
            send_rows(g_own, *groups[chunk + 1][1], *chunks[chunk + 1])
        if chunk + 2 < last:
            send_rows(q_ref, *groups[chunk + 2][0], *chunks[chunk + 2])
        if chunk > 0:
            chunk_far(chunk - 1)
        chunk_logs(chunk)
        chunk_own(chunk)
    chunk_far(last - 1)

    def write_keys(head, carry):
        cols = head_cols(head)
        dk_ref[:, cols] = dk_acc[head].astype(jnp.bfloat16)
        dv_ref[:, cols] = (dv_acc[head] * math.sqrt(HD)).astype(jnp.bfloat16)
        return carry

    lax.fori_loop(0, heads, write_keys, 0)

    def all_sent():
        def head_sent(step, carry):
            head_copy(lax.rem(hx + step, nh), hx).wait_send()
            return carry

        lax.fori_loop(1, nh, head_sent, 0)
        for rows, grads, stats, logs, parts in groups:
            sent_down(*rows)
            sent_down(*grads)
            sent_up(*stats)
            sent_down(*logs)
            sent_up(*parts)

    def chunk_queries(chunk):
        (start, stop), parts = chunks[chunk], groups[chunk][4]
        wait_near(*parts)

        def write_queries(row, carry):
            place = pl.ds(pl.multiple_of(row * QCHUNK, QCHUNK), QCHUNK)
            for local in range(stop - start):
                total = dq_own[start + local, place]
                for pick in range(3):
                    live = jnp.full((QCHUNK, HD), own_live[row * 3 + pick], jnp.int32) > 0
                    far = parts[1][own_pick[row * 3 + pick], local].astype(jnp.float32)
                    total += jnp.where(live, far, 0.0)
                dq_ref[place, pl.ds((start + local) * HD, HD)] = total.astype(jnp.bfloat16)
            return carry

        lax.fori_loop(0, stretches, write_queries, 0)

    for chunk in range(last - 1):
        chunk_queries(chunk)
    all_sent()
    chunk_queries(last - 1)


def attention_grads(n, nh, tables, queries, keys, values, out_grad):
    block, feats = queries.shape
    heads = feats // HD
    chunks = head_chunks(heads)
    stretches = block // QCHUNK
    bf, f32 = jnp.bfloat16, jnp.float32
    dma = pltpu.SemaphoreType.DMA
    most = max(stop - start for start, stop in chunks)
    scratch = [
        pltpu.VMEM((stretches, QCHUNK, feats), bf),
        pltpu.VMEM((heads, HD, block), bf),
        pltpu.VMEM((heads, block, HD), f32),
        pltpu.VMEM((heads, block, HD), f32),
        pltpu.VMEM((heads, block, HD), f32),
        pltpu.VMEM((most, 8, n * QCHUNK), f32),
        pltpu.VMEM((heads, 8, block), f32),
        pltpu.VMEM((3, stretches, 128), f32),
        pltpu.VMEM((3, 3, stretches, 128), f32),
        pltpu.VMEM((stretches, 2, 128), f32),
        pltpu.VMEM((most, 8, n * QCHUNK), f32),
        pltpu.VMEM((most, 8, n * QCHUNK), f32),
        pltpu.VMEM((most, 8, block), f32),
        pltpu.VMEM((most, 8, block), f32),
        dma((nh,)),
        dma((nh,)),
    ]
    half = block // 2
    for lead, keys_held, cols_held in (
        ((2, most, n // TILE_SLOTS), block, TILE),
        ((heads,), block, half),
        ((heads,), half, half),
    ):
        scratch += [pltpu.VMEM((*lead, rows, cols_held), f32) for rows in (keys_held, keys_held, 8)]
    for start, stop in chunks:
        row_shape = (n, stop - start, QCHUNK, HD)
        for shape, dtype in (
            (row_shape, bf),
            (row_shape, bf),
            ((n, 8, 128), f32),
            ((n, 2, 128), f32),
            (row_shape, bf),
        ):
            scratch += [pltpu.VMEM(shape, dtype), pltpu.VMEM(shape, dtype), dma((n,)), dma((n,))]
    whole = pl.BlockSpec(memory_space=pltpu.VMEM)
    small = pl.BlockSpec(memory_space=pltpu.SMEM)
    out = jax.ShapeDtypeStruct((block, feats), bf)
    pairs = (n + stretches) // 2 * QCHUNK * block * feats
    return pl.pallas_call(
        functools.partial(kernel, n, nh, heads, chunks),
        out_shape=(out, out, out),
        in_specs=[small] * 4 + [whole] * 4,
        out_specs=(whole, whole, whole),
        scratch_shapes=scratch,
        cost_estimate=pl.CostEstimate(flops=14 * pairs, bytes_accessed=14 * block * feats, transcendentals=0),
        compiler_params=pltpu.CompilerParams(
            collective_id=0, has_side_effects=True, vmem_limit_bytes=60 * 1024 * 1024
        ),
    )(*tables, queries.reshape(stretches, QCHUNK, feats), keys, values, out_grad.reshape(-1, QCHUNK, nh * feats))


def per_device(queries, keys, values, out_grad, selection):
    n = lax.axis_size("seq")
    nh = lax.axis_size("head")
    me = lax.axis_index("seq")
    stretches = queries.shape[0] // QCHUNK
    own = lax.dynamic_slice_in_dim(selection, me * stretches, stretches, 0)
    live = own != me
    peers = jnp.arange(n, dtype=jnp.int32)
    hits = (own[:, :, None] == peers[None, None, :]) & live[:, :, None]
    places = jnp.arange(stretches, dtype=jnp.int32)[:, None, None]
    used = jnp.any(hits, axis=(0, 1)).astype(jnp.int32)
    stretch = jnp.sum(jnp.where(hits, places, 0), axis=(0, 1))
    tables = (
        stretch,
        used,
        jnp.where(live, own, 0).reshape(-1),
        live.astype(jnp.int32).reshape(-1),
    )
    return attention_grads(n, nh, tables, queries, keys, values, out_grad)


def solution(mesh):
    return jax.shard_map(
        per_device,
        mesh=mesh,
        in_specs=(
            P("seq", "head"),
            P("seq", "head"),
            P("seq", "head"),
            P(("seq", "head"), None),
            P(),
        ),
        out_specs=(P("seq", "head"), P("seq", "head"), P("seq", "head")),
        check_vma=False,
    )
```

```python
import functools
import math

import jax
import jax.numpy as jnp
from jax import lax
from jax.experimental import pallas as pl
from jax.experimental.pallas import tpu as pltpu
from jax.sharding import PartitionSpec as P

HD = 128
QCHUNK = 32
TILE_SLOTS = 8
TILE = TILE_SLOTS * QCHUNK
GROUP = 128 // QCHUNK
PIECES = 4
SCALE = 1.0 / math.sqrt(HD)
EXPO = SCALE * math.log2(math.e)
NEG = -1e30
BIG = 1e30
NT_DIMS = (((1,), (1,)), ((), ()))
MESH = pl.DeviceIdType.MESH


def head_chunks(head_count):
    edges = list(range(0, head_count, 2)) + [head_count]
    return tuple(zip(edges[:-1], edges[1:]))


def dot(lhs, rhs):
    return jnp.dot(lhs, rhs, preferred_element_type=jnp.float32)


def dot_nt(lhs, rhs):
    return lax.dot_general(lhs, rhs, NT_DIMS, preferred_element_type=jnp.float32)


def score_columns(key_tile, query_tile, diagonal):
    scores = dot_nt(key_tile, query_tile)
    if diagonal is not None:
        rows = lax.broadcasted_iota(jnp.int32, scores.shape, 0)
        cols = lax.broadcasted_iota(jnp.int32, scores.shape, 1)
        scores = jnp.where(rows <= cols + diagonal, scores, NEG)
    return scores


def stats_tile(key_tile, value_tile, query_tile, grad_tile, diagonal, weight_ref, prob_ref, top_ref):
    scores = score_columns(key_tile, query_tile, diagonal)
    grad_prob = dot_nt(value_tile, grad_tile)
    prob_ref[...] = grad_prob
    rows = scores.shape[0] // PIECES
    tops, totals, inners = [], [], []
    for piece in range(PIECES):
        span = slice(piece * rows, piece * rows + rows)
        top = jnp.max(scores[span], axis=0, keepdims=True)
        weights = jnp.exp2((scores[span] - top) * EXPO)
        weight_ref[span] = weights
        top_ref[piece : piece + 1] = top
        tops.append(top)
        totals.append(jnp.sum(weights, axis=0, keepdims=True))
        inners.append(jnp.sum(weights * grad_prob[span], axis=0, keepdims=True))
    best = functools.reduce(jnp.maximum, tops)
    factors = [jnp.exp2((top - best) * EXPO) for top in tops]
    total = sum(factor * part for factor, part in zip(factors, totals))
    inner = sum(factor * part for factor, part in zip(factors, inners))
    return best, total, inner


def grads_tile(key_t, query_tile, grad_tile, log_row, delta_row, weight_ref, prob_ref, top_ref):
    rows = weight_ref.shape[0] // PIECES
    probs, scores = [], []
    for piece in range(PIECES):
        span = slice(piece * rows, piece * rows + rows)
        prob = weight_ref[span] * jnp.exp2((top_ref[piece : piece + 1] - log_row) * EXPO)
        probs.append(prob.astype(jnp.bfloat16))
        scores.append((prob * (prob_ref[span] - delta_row)).astype(jnp.bfloat16))
    prob_half = jnp.concatenate(probs, axis=0)
    grad_score = jnp.concatenate(scores, axis=0)
    grad_key = dot(grad_score, query_tile)
    grad_value = dot(prob_half, grad_tile)
    grad_query = dot(key_t, grad_score).T
    return grad_query, grad_key, grad_value


def quarter_swap(parts, target):
    lane = lax.broadcasted_iota(jnp.int32, parts[0].shape, 1) // QCHUNK
    out = jnp.zeros(parts[0].shape, jnp.float32)
    for source, part in enumerate(parts):
        shift = ((source - target) * QCHUNK) % 128
        moved = pltpu.roll(part, shift, 1) if shift else part
        out = jnp.where(lane == source, moved, out)
    return out


def kernel(n, nh, heads, chunks, *refs):
    refs = list(refs)
    sent_stretch, sent_used, own_pick, own_live = refs[:4]
    q_ref, k_ref, v_ref, g_ref = refs[4:8]
    dq_ref, dk_ref, dv_ref = refs[8:11]
    g_own, k_t, dk_acc, dv_acc, dq_own = refs[11:16]
    stat_far, stat_own, own_rows, far_rows, logs_own, log_far, delta_far, log_head, delta_head = refs[16:25]
    head_send, head_recv = refs[25:27]
    far_kept, high_kept, low_kept = refs[27:30], refs[30:33], refs[33:36]
    rest = refs[36:]
    buffers = []
    for _ in chunks:
        buffers.append(rest[:20])
        rest = rest[20:]

    me = lax.axis_index("seq")
    hx = lax.axis_index("head")
    stretches = q_ref.shape[0]
    block = stretches * QCHUNK
    feats = heads * HD
    piece = stretches // nh
    tiles = n // TILE_SLOTS
    first_tile = (me + 1) // TILE_SLOTS

    def head_cols(head):
        return pl.ds(pl.multiple_of(head * HD, HD), HD)

    barrier = pltpu.get_barrier_semaphore()

    def greet_seq(step, carry):
        peer = lax.rem(me + step, n)
        pl.semaphore_signal(barrier, inc=1, device_id=(peer, hx), device_id_type=MESH)
        return carry

    def greet_head(step, carry):
        peer = lax.rem(hx + step, nh)
        pl.semaphore_signal(barrier, inc=1, device_id=(me, peer), device_id_type=MESH)
        return carry

    lax.fori_loop(1, n, greet_seq, 0)
    lax.fori_loop(1, nh, greet_head, 0)
    pl.semaphore_wait(barrier, n - 1 + nh - 1)

    def head_copy(peer, slot):
        return pltpu.make_async_remote_copy(
            src_ref=g_ref.at[:, :, pl.ds(pl.multiple_of(peer * feats, HD), feats)],
            dst_ref=g_own.at[pl.ds(slot * piece, piece)],
            send_sem=head_send.at[peer],
            recv_sem=head_recv.at[slot],
            device_id=(me, peer),
            device_id_type=MESH,
        )

    def start_head(step, carry):
        head_copy(lax.rem(hx + step, nh), hx).start()
        return carry

    lax.fori_loop(1, nh, start_head, 0)

    def pair_copy(src, dst, send, recv, peer, slot):
        return pltpu.make_async_remote_copy(
            src_ref=src.at[peer],
            dst_ref=dst.at[slot],
            send_sem=send.at[peer],
            recv_sem=recv.at[slot],
            device_id=(peer, hx),
            device_id_type=MESH,
        )

    def each_near(body):
        def step(i, carry):
            place = me - 1 - i
            hop = place // 2
            body(hop + (place % 2) * (me - 1 - 2 * hop))
            return carry

        lax.fori_loop(0, me, step, 0)

    def each_far(body):
        def step(i, carry):
            place = n - 2 - me - i
            hop = place // 2
            body(n - 1 - hop - (place % 2) * (n - 2 - me - 2 * hop))
            return carry

        lax.fori_loop(0, n - 1 - me, step, 0)

    def start_down(src, dst, send, recv):
        each_near(lambda peer: pair_copy(src, dst, send, recv, peer, me).start())

    def gather_rows(source, kind):
        def body(peer):
            row = sent_stretch[peer]
            for (start, stop), group in zip(chunks, groups):
                for head in range(start, stop):
                    group[kind][0][peer, head - start] = source[row, :, head * HD : head * HD + HD]
            pair_copy(*groups[0][kind], peer, me).start()

        each_near(body)

    def wait_far(src, dst, send, recv):
        def step(peer, carry):
            pair_copy(src, dst, send, recv, peer, peer).wait_recv()
            return carry

        lax.fori_loop(me + 1, n, step, 0)

    def wait_near(src, dst, send, recv):
        def step(peer, carry):
            pair_copy(src, dst, send, recv, peer, peer).wait_recv()
            return carry

        lax.fori_loop(0, me, step, 0)

    def sent_down(src, dst, send, recv):
        def step(peer, carry):
            pair_copy(src, dst, send, recv, peer, me).wait_send()
            return carry

        lax.fori_loop(0, me, step, 0)

    def start_up(src, dst, send, recv):
        each_far(lambda peer: pair_copy(src, dst, send, recv, peer, me).start())

    def sent_up(src, dst, send, recv):
        def step(peer, carry):
            pair_copy(src, dst, send, recv, peer, me).wait_send()
            return carry

        lax.fori_loop(me + 1, n, step, 0)

    groups = []
    for held in buffers:
        groups.append(tuple(tuple(held[4 * i : 4 * i + 4]) for i in range(5)))

    gather_rows(q_ref, 0)
    start_down(*groups[1][0])

    def clear(slot, carry):
        for rows, grads, stats, logs, parts in groups:
            rows[1][slot] = jnp.zeros(rows[1].shape[1:], jnp.bfloat16)
            grads[1][slot] = jnp.zeros(grads[1].shape[1:], jnp.bfloat16)
            logs[1][slot, 0:1] = jnp.full((1, 128), BIG, jnp.float32)
            logs[1][slot, 1:2] = jnp.zeros((1, 128), jnp.float32)
        return carry

    lax.fori_loop(0, me + 1, clear, 0)

    def turn(head, carry):
        k_t[head] = k_ref[:, head_cols(head)].T
        return carry

    lax.fori_loop(0, heads, turn, 0)

    g_own[pl.ds(hx * piece, piece)] = g_ref[:, :, pl.ds(pl.multiple_of(hx * feats, HD), feats)]

    def wait_head(step, carry):
        peer = lax.rem(hx + step, nh)
        head_copy(peer, peer).wait_recv()
        return carry

    lax.fori_loop(1, nh, wait_head, 0)
    gather_rows(g_own, 1)

    half = block // 2
    middle = stretches // 2

    def own_tile(source, upper, cols):
        places = slice(middle, stretches) if upper else slice(0, middle)
        return source[places, :, cols].reshape(half, HD)

    def pad_stats(top, total, inner):
        return jnp.concatenate([top, total, inner, jnp.zeros((5, top.shape[1]), jnp.float32)], axis=0)

    def own_stats(head, carry):
        cols = head_cols(head)
        stat_own[head, :, 0:half] = pad_stats(
            *stats_tile(
                k_ref[0:half, cols], v_ref[0:half, cols], own_tile(q_ref, False, cols), own_tile(g_own, False, cols), 0,
                *(kept.at[head] for kept in low_kept),
            )
        )
        stat_own[head, :, half:block] = pad_stats(
            *stats_tile(
                k_ref[:, cols], v_ref[:, cols], own_tile(q_ref, True, cols), own_tile(g_own, True, cols), half,
                *(kept.at[head] for kept in high_kept),
            )
        )
        return carry

    lax.fori_loop(0, heads, own_stats, 0)
    for chunk, (start, stop) in enumerate(chunks):
        for group in range(stretches // GROUP):
            held = [stat_own[head, :, group * 128 : group * 128 + 128] for head in range(start, stop)]
            for slot in range(GROUP):
                swapped = quarter_swap(held, slot)
                row = group * GROUP + slot
                for kind in range(3):
                    own_rows[chunk, kind, row : row + 1] = swapped[kind : kind + 1]

    def chunk_stats(chunk):
        (start, stop), (rows, grads, stats, logs, parts) = chunks[chunk], groups[chunk]
        count = stop - start
        wait_far(*rows)
        wait_far(*grads)

        def far_stats(tile, carry):
            slots = pl.ds(pl.multiple_of(tile * TILE_SLOTS, TILE_SLOTS), TILE_SLOTS)
            for local in range(count):
                cols = pl.ds((local + start) * HD, HD)
                query_tile = rows[1][slots, local].reshape(TILE, HD)
                grad_tile = grads[1][slots, local].reshape(TILE, HD)
                stat_far[local, :, pl.ds(pl.multiple_of(tile * TILE, TILE), TILE)] = pad_stats(
                    *stats_tile(
                        k_ref[:, cols], v_ref[:, cols], query_tile, grad_tile, None,
                        *(kept.at[chunk % 2, local, tile] for kept in far_kept),
                    )
                )
            return carry

        lax.fori_loop(first_tile, tiles, far_stats, 0)

        def far_swap(group, carry):
            lanes = pl.ds(pl.multiple_of(group * 128, 128), 128)
            held = [stat_far[local, :, lanes] for local in range(count)]
            for slot in range(GROUP):
                stats[0][group * GROUP + slot] = quarter_swap(held, slot)
            return carry

        lax.fori_loop(first_tile * (TILE // 128), n // GROUP, far_swap, 0)
        start_up(*stats)

    def chunk_logs(chunk):
        (start, stop), (rows, grads, stats, logs, parts) = chunks[chunk], groups[chunk]
        count = stop - start
        wait_near(*stats)
        fill = jnp.where(lax.broadcasted_iota(jnp.int32, (8, 128), 0) == 0, NEG, 0.0)
        for row in range(stretches):
            for pick in range(3):
                live = own_live[row * 3 + pick]
                found = jnp.where(jnp.full((8, 128), live, jnp.int32) > 0, stats[1][own_pick[row * 3 + pick]], fill)
                for kind in range(3):
                    far_rows[pick, kind, row : row + 1] = found[kind : kind + 1]
        best = own_rows[chunk, 0]
        for pick in range(3):
            best = jnp.maximum(best, far_rows[pick, 0])
        weight = jnp.exp2((own_rows[chunk, 0] - best) * EXPO)
        total = own_rows[chunk, 1] * weight
        inner = own_rows[chunk, 2] * weight
        for pick in range(3):
            weight = jnp.exp2((far_rows[pick, 0] - best) * EXPO)
            total += far_rows[pick, 1] * weight
            inner += far_rows[pick, 2] * weight
        log_total = best + (jnp.log(total) - math.log(SCALE)) * (1.0 / SCALE)
        delta = inner / total
        for row in range(stretches):
            logs_own[row, 0:1] = log_total[row : row + 1]
            logs_own[row, 1:2] = delta[row : row + 1]

        for peer in range(n - 1):
            row = sent_stretch[peer]
            used = jnp.full((1, 128), sent_used[peer], jnp.int32) > 0
            logs[0][peer, 0:1] = jnp.where(used, logs_own[row, 0:1], BIG)
            logs[0][peer, 1:2] = jnp.where(used, logs_own[row, 1:2], 0.0)
        start_down(*logs)

        for group in range(stretches // GROUP):
            for kind, kept in ((0, log_head), (1, delta_head)):
                lines = [
                    jnp.broadcast_to(logs_own[group * GROUP + slot, kind : kind + 1], (8, 128))
                    for slot in range(GROUP)
                ]
                for local in range(count):
                    kept[local, :, group * 128 : group * 128 + 128] = quarter_swap(lines, local)

    def chunk_own(chunk):
        (start, stop), (rows, grads, stats, logs, parts) = chunks[chunk], groups[chunk]
        count = stop - start
        def own_grads(local, carry):
            head = local + start
            cols = head_cols(head)
            grad_query, grad_key, grad_value = grads_tile(
                k_t[head], own_tile(q_ref, True, cols), own_tile(g_own, True, cols),
                log_head[local, 0:1, half:block], delta_head[local, 0:1, half:block],
                *(kept.at[head] for kept in high_kept),
            )
            dq_own[head, half:block] = grad_query
            dk_acc[head] = grad_key
            dv_acc[head] = grad_value
            grad_query, grad_key, grad_value = grads_tile(
                k_t[head, :, 0:half], own_tile(q_ref, False, cols), own_tile(g_own, False, cols),
                log_head[local, 0:1, 0:half], delta_head[local, 0:1, 0:half],
                *(kept.at[head] for kept in low_kept),
            )
            dq_own[head, 0:half] = grad_query
            dk_acc[head, 0:half] += grad_key
            dv_acc[head, 0:half] += grad_value
            return carry

        lax.fori_loop(0, count, own_grads, 0)

    def chunk_far(chunk):
        (start, stop), (rows, grads, stats, logs, parts) = chunks[chunk], groups[chunk]
        count = stop - start
        wait_far(*logs)

        def far_logs(group, carry):
            lanes = pl.ds(pl.multiple_of(group * 128, 128), 128)
            for kind, kept in ((0, log_far), (1, delta_far)):
                lines = [
                    jnp.broadcast_to(logs[1][group * GROUP + slot, kind : kind + 1], (8, 128)) for slot in range(GROUP)
                ]
                for local in range(count):
                    kept[local, :, lanes] = quarter_swap(lines, local)
            return carry

        lax.fori_loop(first_tile * (TILE // 128), n // GROUP, far_logs, 0)

        def far_grads(tile, carry):
            slots = pl.ds(pl.multiple_of(tile * TILE_SLOTS, TILE_SLOTS), TILE_SLOTS)
            lanes = pl.ds(pl.multiple_of(tile * TILE, TILE), TILE)
            for local in range(count):
                head = local + start
                query_tile = rows[1][slots, local].reshape(TILE, HD)
                grad_tile = grads[1][slots, local].reshape(TILE, HD)
                grad_query, grad_key, grad_value = grads_tile(
                    k_t[head], query_tile, grad_tile, log_far[local, 0:1, lanes], delta_far[local, 0:1, lanes],
                    *(kept.at[chunk % 2, local, tile] for kept in far_kept),
                )
                parts[0][slots, local] = grad_query.astype(jnp.bfloat16).reshape(TILE_SLOTS, QCHUNK, HD)
                dk_acc[head] += grad_key
                dv_acc[head] += grad_value
            return carry

        lax.fori_loop(first_tile, tiles, far_grads, 0)
        start_up(*parts)

    last = len(chunks)
    for chunk in range(last):
        chunk_stats(chunk)
        if chunk + 1 < last:
            start_down(*groups[chunk + 1][1])
        if chunk + 2 < last:
            start_down(*groups[chunk + 2][0])
        if chunk > 0:
            chunk_far(chunk - 1)
        chunk_logs(chunk)
        chunk_own(chunk)
    chunk_far(last - 1)

    def write_keys(head, carry):
        cols = head_cols(head)
        dk_ref[:, cols] = dk_acc[head].astype(jnp.bfloat16)
        dv_ref[:, cols] = (dv_acc[head] * math.sqrt(HD)).astype(jnp.bfloat16)
        return carry

    lax.fori_loop(0, heads, write_keys, 0)

    def all_sent():
        def head_sent(step, carry):
            head_copy(lax.rem(hx + step, nh), hx).wait_send()
            return carry

        lax.fori_loop(1, nh, head_sent, 0)
        for rows, grads, stats, logs, parts in groups:
            sent_down(*rows)
            sent_down(*grads)
            sent_up(*stats)
            sent_down(*logs)
            sent_up(*parts)

    def chunk_queries(chunk):
        (start, stop), parts = chunks[chunk], groups[chunk][4]
        wait_near(*parts)

        def write_queries(row, carry):
            place = pl.ds(pl.multiple_of(row * QCHUNK, QCHUNK), QCHUNK)
            for local in range(stop - start):
                total = dq_own[start + local, place]
                for pick in range(3):
                    live = jnp.full((QCHUNK, HD), own_live[row * 3 + pick], jnp.int32) > 0
                    far = parts[1][own_pick[row * 3 + pick], local].astype(jnp.float32)
                    total += jnp.where(live, far, 0.0)
                dq_ref[place, pl.ds((start + local) * HD, HD)] = total.astype(jnp.bfloat16)
            return carry

        lax.fori_loop(0, stretches, write_queries, 0)

    for chunk in range(last - 1):
        chunk_queries(chunk)
    all_sent()
    chunk_queries(last - 1)


def attention_grads(n, nh, tables, queries, keys, values, out_grad):
    block, feats = queries.shape
    heads = feats // HD
    chunks = head_chunks(heads)
    stretches = block // QCHUNK
    bf, f32 = jnp.bfloat16, jnp.float32
    dma = pltpu.SemaphoreType.DMA
    most = max(stop - start for start, stop in chunks)
    scratch = [
        pltpu.VMEM((stretches, QCHUNK, feats), bf),
        pltpu.VMEM((heads, HD, block), bf),
        pltpu.VMEM((heads, block, HD), f32),
        pltpu.VMEM((heads, block, HD), f32),
        pltpu.VMEM((heads, block, HD), f32),
        pltpu.VMEM((most, 8, n * QCHUNK), f32),
        pltpu.VMEM((heads, 8, block), f32),
        pltpu.VMEM((len(chunks), 3, stretches, 128), f32),
        pltpu.VMEM((3, 3, stretches, 128), f32),
        pltpu.VMEM((stretches, 2, 128), f32),
        pltpu.VMEM((most, 8, n * QCHUNK), f32),
        pltpu.VMEM((most, 8, n * QCHUNK), f32),
        pltpu.VMEM((most, 8, block), f32),
        pltpu.VMEM((most, 8, block), f32),
        dma((nh,)),
        dma((nh,)),
    ]
    half = block // 2
    for lead, keys_held, cols_held in (
        ((2, most, n // TILE_SLOTS), block, TILE),
        ((heads,), block, half),
        ((heads,), half, half),
    ):
        scratch += [pltpu.VMEM((*lead, rows, cols_held), f32) for rows in (keys_held, keys_held, 8)]
    for start, stop in chunks:
        row_shape = (n, stop - start, QCHUNK, HD)
        for shape, dtype in (
            (row_shape, bf),
            (row_shape, bf),
            ((n, 8, 128), f32),
            ((n, 2, 128), f32),
            (row_shape, bf),
        ):
            scratch += [pltpu.VMEM(shape, dtype), pltpu.VMEM(shape, dtype), dma((n,)), dma((n,))]
    whole = pl.BlockSpec(memory_space=pltpu.VMEM)
    small = pl.BlockSpec(memory_space=pltpu.SMEM)
    out = jax.ShapeDtypeStruct((block, feats), bf)
    pairs = (n + stretches) // 2 * QCHUNK * block * feats
    return pl.pallas_call(
        functools.partial(kernel, n, nh, heads, chunks),
        out_shape=(out, out, out),
        in_specs=[small] * 4 + [whole] * 4,
        out_specs=(whole, whole, whole),
        scratch_shapes=scratch,
        cost_estimate=pl.CostEstimate(flops=14 * pairs, bytes_accessed=14 * block * feats, transcendentals=0),
        compiler_params=pltpu.CompilerParams(
            collective_id=0, has_side_effects=True, vmem_limit_bytes=60 * 1024 * 1024
        ),
    )(*tables, queries.reshape(stretches, QCHUNK, feats), keys, values, out_grad.reshape(-1, QCHUNK, nh * feats))


def per_device(queries, keys, values, out_grad, selection):
    n = lax.axis_size("seq")
    nh = lax.axis_size("head")
    me = lax.axis_index("seq")
    stretches = queries.shape[0] // QCHUNK
    own = lax.dynamic_slice_in_dim(selection, me * stretches, stretches, 0)
    live = own != me
    peers = jnp.arange(n, dtype=jnp.int32)
    hits = (own[:, :, None] == peers[None, None, :]) & live[:, :, None]
    places = jnp.arange(stretches, dtype=jnp.int32)[:, None, None]
    used = jnp.any(hits, axis=(0, 1)).astype(jnp.int32)
    stretch = jnp.sum(jnp.where(hits, places, 0), axis=(0, 1))
    tables = (
        stretch,
        used,
        jnp.where(live, own, 0).reshape(-1),
        live.astype(jnp.int32).reshape(-1),
    )
    return attention_grads(n, nh, tables, queries, keys, values, out_grad)


def solution(mesh):
    return jax.shard_map(
        per_device,
        mesh=mesh,
        in_specs=(
            P("seq", "head"),
            P("seq", "head"),
            P("seq", "head"),
            P(("seq", "head"), None),
            P(),
        ),
        out_specs=(P("seq", "head"), P("seq", "head"), P("seq", "head")),
        check_vma=False,
    )
```

```python
import functools
import math

import jax
import jax.numpy as jnp
from jax import lax
from jax.experimental import pallas as pl
from jax.experimental.pallas import tpu as pltpu
from jax.sharding import PartitionSpec as P

HD = 128
QCHUNK = 32
TILE_SLOTS = 8
TILE = TILE_SLOTS * QCHUNK
GROUP = 128 // QCHUNK
PIECES = 4
SCALE = 1.0 / math.sqrt(HD)
EXPO = SCALE * math.log2(math.e)
NEG = -1e30
BIG = 1e30
NT_DIMS = (((1,), (1,)), ((), ()))
MESH = pl.DeviceIdType.MESH


def head_chunks(head_count):
    edges = list(range(0, head_count, 2)) + [head_count]
    return tuple(zip(edges[:-1], edges[1:]))


def dot(lhs, rhs):
    return jnp.dot(lhs, rhs, preferred_element_type=jnp.float32)


def dot_nt(lhs, rhs):
    return lax.dot_general(lhs, rhs, NT_DIMS, preferred_element_type=jnp.float32)


def score_columns(key_tile, query_tile, diagonal):
    scores = dot_nt(key_tile, query_tile)
    if diagonal is not None:
        rows = lax.broadcasted_iota(jnp.int32, scores.shape, 0)
        cols = lax.broadcasted_iota(jnp.int32, scores.shape, 1)
        scores = jnp.where(rows <= cols + diagonal, scores, NEG)
    return scores


def stats_tile(key_tile, value_tile, query_tile, grad_tile, diagonal, weight_ref, prob_ref, top_ref):
    scores = score_columns(key_tile, query_tile, diagonal)
    grad_prob = dot_nt(value_tile, grad_tile)
    prob_ref[...] = grad_prob
    rows = scores.shape[0] // PIECES
    tops, totals, inners = [], [], []
    for piece in range(PIECES):
        span = slice(piece * rows, piece * rows + rows)
        top = jnp.max(scores[span], axis=0, keepdims=True)
        weights = jnp.exp2((scores[span] - top) * EXPO)
        weight_ref[span] = weights
        top_ref[piece : piece + 1] = top
        tops.append(top)
        totals.append(jnp.sum(weights, axis=0, keepdims=True))
        inners.append(jnp.sum(weights * grad_prob[span], axis=0, keepdims=True))
    best = functools.reduce(jnp.maximum, tops)
    factors = [jnp.exp2((top - best) * EXPO) for top in tops]
    total = sum(factor * part for factor, part in zip(factors, totals))
    inner = sum(factor * part for factor, part in zip(factors, inners))
    return best, total, inner


def grads_tile(key_t, query_tile, grad_tile, log_row, delta_row, weight_ref, prob_ref, top_ref):
    rows = weight_ref.shape[0] // PIECES
    probs, scores = [], []
    for piece in range(PIECES):
        span = slice(piece * rows, piece * rows + rows)
        prob = weight_ref[span] * jnp.exp2((top_ref[piece : piece + 1] - log_row) * EXPO)
        probs.append(prob.astype(jnp.bfloat16))
        scores.append((prob * (prob_ref[span] - delta_row)).astype(jnp.bfloat16))
    prob_half = jnp.concatenate(probs, axis=0)
    grad_score = jnp.concatenate(scores, axis=0)
    grad_key = dot(grad_score, query_tile)
    grad_value = dot(prob_half, grad_tile)
    grad_query = dot(key_t, grad_score).T
    return grad_query, grad_key, grad_value


def quarter_swap(parts, target):
    lane = lax.broadcasted_iota(jnp.int32, parts[0].shape, 1) // QCHUNK
    out = jnp.zeros(parts[0].shape, jnp.float32)
    for source, part in enumerate(parts):
        shift = ((source - target) * QCHUNK) % 128
        moved = pltpu.roll(part, shift, 1) if shift else part
        out = jnp.where(lane == source, moved, out)
    return out


def kernel(n, nh, heads, chunks, *refs):
    refs = list(refs)
    sent_code, own_list = refs[:2]
    refs = refs[2:]
    q_ref, k_ref, v_ref, g_ref = refs[:4]
    dq_ref, dk_ref, dv_ref = refs[4:7]
    g_own, k_t, dk_acc, dv_acc, dq_own = refs[7:12]
    stat_far, stat_own, own_rows, far_rows, logs_own, log_far, delta_far, log_head, delta_head = refs[12:21]
    head_send, head_recv = refs[21:23]
    far_kept, high_kept, low_kept = refs[23:26], refs[26:29], refs[29:32]
    rest = refs[32:]
    buffers = []
    for _ in chunks:
        buffers.append(rest[:20])
        rest = rest[20:]

    me = lax.axis_index("seq")
    hx = lax.axis_index("head")
    stretches = q_ref.shape[0]
    block = stretches * QCHUNK
    feats = heads * HD
    piece = stretches // nh
    tiles = n // TILE_SLOTS
    first_tile = (me + 1) // TILE_SLOTS

    def head_cols(head):
        return pl.ds(pl.multiple_of(head * HD, HD), HD)

    barrier = pltpu.get_barrier_semaphore()

    def greet_seq(step, carry):
        peer = lax.rem(me + step, n)
        pl.semaphore_signal(barrier, inc=1, device_id=(peer, hx), device_id_type=MESH)
        return carry

    def greet_head(step, carry):
        peer = lax.rem(hx + step, nh)
        pl.semaphore_signal(barrier, inc=1, device_id=(me, peer), device_id_type=MESH)
        return carry

    lax.fori_loop(1, n, greet_seq, 0)
    lax.fori_loop(1, nh, greet_head, 0)
    pl.semaphore_wait(barrier, n - 1 + nh - 1)

    def head_copy(peer, slot):
        return pltpu.make_async_remote_copy(
            src_ref=g_ref.at[:, :, pl.ds(pl.multiple_of(peer * feats, HD), feats)],
            dst_ref=g_own.at[pl.ds(slot * piece, piece)],
            send_sem=head_send.at[peer],
            recv_sem=head_recv.at[slot],
            device_id=(me, peer),
            device_id_type=MESH,
        )

    def start_head(step, carry):
        head_copy(lax.rem(hx + step, nh), hx).start()
        return carry

    lax.fori_loop(1, nh, start_head, 0)

    def pair_copy(src, dst, send, recv, peer, slot):
        return pltpu.make_async_remote_copy(
            src_ref=src.at[peer],
            dst_ref=dst.at[slot],
            send_sem=send.at[peer],
            recv_sem=recv.at[slot],
            device_id=(peer, hx),
            device_id_type=MESH,
        )

    def each_near(body):
        def step(i, carry):
            place = me - 1 - i
            hop = place // 2
            body(hop + (place % 2) * (me - 1 - 2 * hop))
            return carry

        lax.fori_loop(0, me, step, 0)

    def each_far(body):
        def step(i, carry):
            place = n - 2 - me - i
            hop = place // 2
            body(n - 1 - hop - (place % 2) * (n - 2 - me - 2 * hop))
            return carry

        lax.fori_loop(0, n - 1 - me, step, 0)

    def start_down(src, dst, send, recv):
        each_near(lambda peer: pair_copy(src, dst, send, recv, peer, me).start())

    def gather_rows(source, kind):
        def body(peer):
            row = jnp.maximum(sent_code[peer] - 1, 0)
            for (start, stop), group in zip(chunks, groups):
                for head in range(start, stop):
                    group[kind][0][peer, head - start] = source[row, :, head * HD : head * HD + HD]
            pair_copy(*groups[0][kind], peer, me).start()

        each_near(body)

    def wait_far(src, dst, send, recv):
        def step(peer, carry):
            pair_copy(src, dst, send, recv, peer, peer).wait_recv()
            return carry

        lax.fori_loop(me + 1, n, step, 0)

    def wait_near(src, dst, send, recv):
        def step(peer, carry):
            pair_copy(src, dst, send, recv, peer, peer).wait_recv()
            return carry

        lax.fori_loop(0, me, step, 0)

    def sent_down(src, dst, send, recv):
        def step(peer, carry):
            pair_copy(src, dst, send, recv, peer, me).wait_send()
            return carry

        lax.fori_loop(0, me, step, 0)

    def start_up(src, dst, send, recv):
        each_far(lambda peer: pair_copy(src, dst, send, recv, peer, me).start())

    def sent_up(src, dst, send, recv):
        def step(peer, carry):
            pair_copy(src, dst, send, recv, peer, me).wait_send()
            return carry

        lax.fori_loop(me + 1, n, step, 0)

    groups = []
    for held in buffers:
        groups.append(tuple(tuple(held[4 * i : 4 * i + 4]) for i in range(5)))

    gather_rows(q_ref, 0)
    start_down(*groups[1][0])

    def clear(slot, carry):
        for rows, grads, stats, logs, parts in groups:
            rows[1][slot] = jnp.zeros(rows[1].shape[1:], jnp.bfloat16)
            grads[1][slot] = jnp.zeros(grads[1].shape[1:], jnp.bfloat16)
            logs[1][slot, 0:1] = jnp.full((1, 128), BIG, jnp.float32)
            logs[1][slot, 1:2] = jnp.zeros((1, 128), jnp.float32)
        return carry

    lax.fori_loop(0, me + 1, clear, 0)

    def turn(head, carry):
        k_t[head] = k_ref[:, head_cols(head)].T
        return carry

    lax.fori_loop(0, heads, turn, 0)

    g_own[pl.ds(hx * piece, piece)] = g_ref[:, :, pl.ds(pl.multiple_of(hx * feats, HD), feats)]

    def wait_head(step, carry):
        peer = lax.rem(hx + step, nh)
        head_copy(peer, peer).wait_recv()
        return carry

    lax.fori_loop(1, nh, wait_head, 0)
    gather_rows(g_own, 1)

    half = block // 2
    middle = stretches // 2

    def own_tile(source, upper, cols):
        places = slice(middle, stretches) if upper else slice(0, middle)
        return source[places, :, cols].reshape(half, HD)

    def pad_stats(top, total, inner):
        return jnp.concatenate([top, total, inner, jnp.zeros((5, top.shape[1]), jnp.float32)], axis=0)

    def own_stats(head, carry):
        cols = head_cols(head)
        stat_own[head, :, 0:half] = pad_stats(
            *stats_tile(
                k_ref[0:half, cols], v_ref[0:half, cols], own_tile(q_ref, False, cols), own_tile(g_own, False, cols), 0,
                *(kept.at[head] for kept in low_kept),
            )
        )
        stat_own[head, :, half:block] = pad_stats(
            *stats_tile(
                k_ref[:, cols], v_ref[:, cols], own_tile(q_ref, True, cols), own_tile(g_own, True, cols), half,
                *(kept.at[head] for kept in high_kept),
            )
        )
        return carry

    lax.fori_loop(0, heads, own_stats, 0)
    for chunk, (start, stop) in enumerate(chunks):
        for group in range(stretches // GROUP):
            held = [stat_own[head, :, group * 128 : group * 128 + 128] for head in range(start, stop)]
            for slot in range(GROUP):
                swapped = quarter_swap(held, slot)
                row = group * GROUP + slot
                for kind in range(3):
                    own_rows[chunk, kind, row : row + 1] = swapped[kind : kind + 1]

    last = len(chunks)
    low_lanes = lax.broadcasted_iota(jnp.int32, (1, 128), 1) < 64

    def chunk_stats(chunk):
        (start, stop), (rows, grads, stats, logs, parts) = chunks[chunk], groups[chunk]
        count = stop - start
        wait_far(*rows)
        wait_far(*grads)

        def far_stats(tile, carry):
            slots = pl.ds(pl.multiple_of(tile * TILE_SLOTS, TILE_SLOTS), TILE_SLOTS)
            for local in range(count):
                cols = pl.ds((local + start) * HD, HD)
                query_tile = rows[1][slots, local].reshape(TILE, HD)
                grad_tile = grads[1][slots, local].reshape(TILE, HD)
                stat_far[local, :, pl.ds(pl.multiple_of(tile * TILE, TILE), TILE)] = pad_stats(
                    *stats_tile(
                        k_ref[:, cols], v_ref[:, cols], query_tile, grad_tile, None,
                        *(kept.at[chunk % 2, local, tile] for kept in far_kept),
                    )
                )
            return carry

        lax.fori_loop(first_tile, tiles, far_stats, 0)

        def far_swap(group, carry):
            lanes = pl.ds(pl.multiple_of(group * 128, 128), 128)
            held = [stat_far[local, :, lanes] for local in range(count)]
            for slot in range(GROUP):
                swapped = quarter_swap(held, slot)
                moved = pltpu.roll(swapped, 64, 1)
                stats[0][group * GROUP + slot, 0:1] = jnp.where(low_lanes, swapped[0:1], moved[1:2])
                stats[0][group * GROUP + slot, 1:2] = swapped[2:3]
            return carry

        lax.fori_loop(first_tile * (TILE // 128), n // GROUP, far_swap, 0)
        start_up(*stats)

    def chunk_logs(chunk):
        (start, stop), (rows, grads, stats, logs, parts) = chunks[chunk], groups[chunk]
        count = stop - start
        wait_near(*stats)
        fill = jnp.where(low_lanes, NEG, 0.0)
        for row in range(stretches):
            for pick in range(3):
                source = own_list[row * 3 + pick]
                live = jnp.full((1, 128), source, jnp.int32) != me
                far_rows[pick, 0, row : row + 1] = jnp.where(live, stats[1][source, 0:1], fill)
                far_rows[pick, 2, row : row + 1] = jnp.where(live, stats[1][source, 1:2], 0.0)
        for pick in range(3):
            far_rows[pick, 1] = pltpu.roll(far_rows[pick, 0], 64, 1)
        best = own_rows[chunk, 0]
        for pick in range(3):
            best = jnp.maximum(best, far_rows[pick, 0])
        weight = jnp.exp2((own_rows[chunk, 0] - best) * EXPO)
        total = own_rows[chunk, 1] * weight
        inner = own_rows[chunk, 2] * weight
        for pick in range(3):
            weight = jnp.exp2((far_rows[pick, 0] - best) * EXPO)
            total += far_rows[pick, 1] * weight
            inner += far_rows[pick, 2] * weight
        log_total = best + (jnp.log(total) - math.log(SCALE)) * (1.0 / SCALE)
        delta = inner / total
        for row in range(stretches):
            logs_own[row, 0:1] = log_total[row : row + 1]
            logs_own[row, 1:2] = delta[row : row + 1]

        for peer in range(n - 1):
            row = jnp.maximum(sent_code[peer] - 1, 0)
            used = jnp.full((1, 128), sent_code[peer], jnp.int32) > 0
            logs[0][peer, 0:1] = jnp.where(used, logs_own[row, 0:1], BIG)
            logs[0][peer, 1:2] = jnp.where(used, logs_own[row, 1:2], 0.0)
        start_down(*logs)

        for group in range(stretches // GROUP):
            for kind, kept in ((0, log_head), (1, delta_head)):
                lines = [
                    jnp.broadcast_to(logs_own[group * GROUP + slot, kind : kind + 1], (8, 128))
                    for slot in range(GROUP)
                ]
                for local in range(count):
                    kept[local, :, group * 128 : group * 128 + 128] = quarter_swap(lines, local)

    def chunk_own(chunk):
        (start, stop), (rows, grads, stats, logs, parts) = chunks[chunk], groups[chunk]
        count = stop - start
        def own_grads(local, carry):
            head = local + start
            cols = head_cols(head)
            grad_query, grad_key, grad_value = grads_tile(
                k_t[head], own_tile(q_ref, True, cols), own_tile(g_own, True, cols),
                log_head[local, 0:1, half:block], delta_head[local, 0:1, half:block],
                *(kept.at[head] for kept in high_kept),
            )
            dq_own[head, half:block] = grad_query
            dk_acc[head] = grad_key
            dv_acc[head] = grad_value
            grad_query, grad_key, grad_value = grads_tile(
                k_t[head, :, 0:half], own_tile(q_ref, False, cols), own_tile(g_own, False, cols),
                log_head[local, 0:1, 0:half], delta_head[local, 0:1, 0:half],
                *(kept.at[head] for kept in low_kept),
            )
            dq_own[head, 0:half] = grad_query
            dk_acc[head, 0:half] += grad_key
            dv_acc[head, 0:half] += grad_value
            return carry

        lax.fori_loop(0, count, own_grads, 0)

    def chunk_far(chunk):
        (start, stop), (rows, grads, stats, logs, parts) = chunks[chunk], groups[chunk]
        count = stop - start
        wait_far(*logs)

        def far_logs(group, carry):
            lanes = pl.ds(pl.multiple_of(group * 128, 128), 128)
            for kind, kept in ((0, log_far), (1, delta_far)):
                lines = [
                    jnp.broadcast_to(logs[1][group * GROUP + slot, kind : kind + 1], (8, 128)) for slot in range(GROUP)
                ]
                for local in range(count):
                    kept[local, :, lanes] = quarter_swap(lines, local)
            return carry

        lax.fori_loop(first_tile * (TILE // 128), n // GROUP, far_logs, 0)

        def far_grads(tile, carry):
            slots = pl.ds(pl.multiple_of(tile * TILE_SLOTS, TILE_SLOTS), TILE_SLOTS)
            lanes = pl.ds(pl.multiple_of(tile * TILE, TILE), TILE)
            for local in range(count):
                head = local + start
                query_tile = rows[1][slots, local].reshape(TILE, HD)
                grad_tile = grads[1][slots, local].reshape(TILE, HD)
                grad_query, grad_key, grad_value = grads_tile(
                    k_t[head], query_tile, grad_tile, log_far[local, 0:1, lanes], delta_far[local, 0:1, lanes],
                    *(kept.at[chunk % 2, local, tile] for kept in far_kept),
                )
                parts[0][slots, local] = grad_query.astype(jnp.bfloat16).reshape(TILE_SLOTS, QCHUNK, HD)
                dk_acc[head] += grad_key
                dv_acc[head] += grad_value
            return carry

        lax.fori_loop(first_tile, tiles, far_grads, 0)
        start_up(*parts)

    for chunk in range(last):
        chunk_stats(chunk)
        if chunk + 1 < last:
            start_down(*groups[chunk + 1][1])
        if chunk + 2 < last:
            start_down(*groups[chunk + 2][0])
        if chunk > 0:
            chunk_far(chunk - 1)
        chunk_logs(chunk)
        chunk_own(chunk)
    chunk_far(last - 1)

    def write_keys(head, carry):
        cols = head_cols(head)
        dk_ref[:, cols] = dk_acc[head].astype(jnp.bfloat16)
        dv_ref[:, cols] = (dv_acc[head] * math.sqrt(HD)).astype(jnp.bfloat16)
        return carry

    lax.fori_loop(0, heads, write_keys, 0)

    def all_sent():
        def head_sent(step, carry):
            head_copy(lax.rem(hx + step, nh), hx).wait_send()
            return carry

        lax.fori_loop(1, nh, head_sent, 0)
        for rows, grads, stats, logs, parts in groups:
            sent_down(*rows)
            sent_down(*grads)
            sent_up(*stats)
            sent_down(*logs)
            sent_up(*parts)

    def chunk_queries(chunk):
        (start, stop), parts = chunks[chunk], groups[chunk][4]
        wait_near(*parts)

        def write_queries(row, carry):
            place = pl.ds(pl.multiple_of(row * QCHUNK, QCHUNK), QCHUNK)
            for local in range(stop - start):
                total = dq_own[start + local, place]
                for pick in range(3):
                    source = own_list[row * 3 + pick]
                    live = jnp.full((QCHUNK, HD), source, jnp.int32) != me
                    far = parts[1][source, local].astype(jnp.float32)
                    total += jnp.where(live, far, 0.0)
                dq_ref[place, pl.ds((start + local) * HD, HD)] = total.astype(jnp.bfloat16)
            return carry

        lax.fori_loop(0, stretches, write_queries, 0)

    for chunk in range(last - 1):
        chunk_queries(chunk)
    all_sent()
    chunk_queries(last - 1)


def attention_grads(n, nh, tables, queries, keys, values, out_grad):
    block, feats = queries.shape
    heads = feats // HD
    chunks = head_chunks(heads)
    stretches = block // QCHUNK
    bf, f32 = jnp.bfloat16, jnp.float32
    dma = pltpu.SemaphoreType.DMA
    most = max(stop - start for start, stop in chunks)
    scratch = [
        pltpu.VMEM((stretches, QCHUNK, feats), bf),
        pltpu.VMEM((heads, HD, block), bf),
        pltpu.VMEM((heads, block, HD), f32),
        pltpu.VMEM((heads, block, HD), f32),
        pltpu.VMEM((heads, block, HD), f32),
        pltpu.VMEM((most, 8, n * QCHUNK), f32),
        pltpu.VMEM((heads, 8, block), f32),
        pltpu.VMEM((len(chunks), 3, stretches, 128), f32),
        pltpu.VMEM((3, 3, stretches, 128), f32),
        pltpu.VMEM((stretches, 2, 128), f32),
        pltpu.VMEM((most, 8, n * QCHUNK), f32),
        pltpu.VMEM((most, 8, n * QCHUNK), f32),
        pltpu.VMEM((most, 8, block), f32),
        pltpu.VMEM((most, 8, block), f32),
        dma((nh,)),
        dma((nh,)),
    ]
    half = block // 2
    for lead, keys_held, cols_held in (
        ((2, most, n // TILE_SLOTS), block, TILE),
        ((heads,), block, half),
        ((heads,), half, half),
    ):
        scratch += [pltpu.VMEM((*lead, rows, cols_held), f32) for rows in (keys_held, keys_held, 8)]
    for start, stop in chunks:
        row_shape = (n, stop - start, QCHUNK, HD)
        for shape, dtype in (
            (row_shape, bf),
            (row_shape, bf),
            ((n, 2, 128), f32),
            ((n, 2, 128), f32),
            (row_shape, bf),
        ):
            scratch += [pltpu.VMEM(shape, dtype), pltpu.VMEM(shape, dtype), dma((n,)), dma((n,))]
    whole = pl.BlockSpec(memory_space=pltpu.VMEM)
    small = pl.BlockSpec(memory_space=pltpu.SMEM)
    out = jax.ShapeDtypeStruct((block, feats), bf)
    pairs = (n + stretches) // 2 * QCHUNK * block * feats
    return pl.pallas_call(
        functools.partial(kernel, n, nh, heads, chunks),
        out_shape=(out, out, out),
        in_specs=[small] * 2 + [whole] * 4,
        out_specs=(whole, whole, whole),
        scratch_shapes=scratch,
        cost_estimate=pl.CostEstimate(flops=14 * pairs, bytes_accessed=14 * block * feats, transcendentals=0),
        compiler_params=pltpu.CompilerParams(
            collective_id=0, has_side_effects=True, vmem_limit_bytes=60 * 1024 * 1024
        ),
    )(*tables, queries.reshape(stretches, QCHUNK, feats), keys, values, out_grad.reshape(-1, QCHUNK, nh * feats))


def per_device(queries, keys, values, out_grad, selection):
    n = lax.axis_size("seq")
    nh = lax.axis_size("head")
    me = lax.axis_index("seq")
    stretches = queries.shape[0] // QCHUNK
    own = lax.dynamic_slice_in_dim(selection, me * stretches, stretches, 0)
    hits = (own[:, :, None] == jnp.arange(n, dtype=jnp.int32)) & (own != me)[:, :, None]
    places = jnp.arange(1, stretches + 1, dtype=jnp.int32)[:, None, None]
    tables = (jnp.sum(jnp.where(hits, places, 0), axis=(0, 1)), own.reshape(-1))
    return attention_grads(n, nh, tables, queries, keys, values, out_grad)


def solution(mesh):
    return jax.shard_map(
        per_device,
        mesh=mesh,
        in_specs=(
            P("seq", "head"),
            P("seq", "head"),
            P("seq", "head"),
            P(("seq", "head"), None),
            P(),
        ),
        out_specs=(P("seq", "head"), P("seq", "head"), P("seq", "head")),
        check_vma=False,
    )
```

```python
import functools
import math

import jax
import jax.numpy as jnp
from jax import lax
from jax.experimental import pallas as pl
from jax.experimental.pallas import tpu as pltpu
from jax.sharding import PartitionSpec as P

HD = 128
QCHUNK = 32
TILE_SLOTS = 8
TILE = TILE_SLOTS * QCHUNK
GROUP = 128 // QCHUNK
PIECES = 4
SCALE = 1.0 / math.sqrt(HD)
EXPO = SCALE * math.log2(math.e)
NEG = -1e30
BIG = 1e30
NT_DIMS = (((1,), (1,)), ((), ()))
MESH = pl.DeviceIdType.MESH


def head_chunks(head_count):
    edges = list(range(0, head_count, 2)) + [head_count]
    return tuple(zip(edges[:-1], edges[1:]))


def dot(lhs, rhs):
    return jnp.dot(lhs, rhs, preferred_element_type=jnp.float32)


def dot_nt(lhs, rhs):
    return lax.dot_general(lhs, rhs, NT_DIMS, preferred_element_type=jnp.float32)


def score_columns(key_tile, query_tile, diagonal):
    scores = dot_nt(key_tile, query_tile)
    if diagonal is not None:
        rows = lax.broadcasted_iota(jnp.int32, scores.shape, 0)
        cols = lax.broadcasted_iota(jnp.int32, scores.shape, 1)
        scores = jnp.where(rows <= cols + diagonal, scores, NEG)
    return scores


def stats_tile(key_tile, value_tile, query_tile, grad_tile, diagonal, weight_ref, prob_ref, top_ref):
    scores = score_columns(key_tile, query_tile, diagonal)
    grad_prob = dot_nt(value_tile, grad_tile)
    prob_ref[...] = grad_prob
    rows = scores.shape[0] // PIECES
    tops, totals, inners = [], [], []
    for piece in range(PIECES):
        span = slice(piece * rows, piece * rows + rows)
        top = jnp.max(scores[span], axis=0, keepdims=True)
        weights = jnp.exp2((scores[span] - top) * EXPO)
        weight_ref[span] = weights
        top_ref[piece : piece + 1] = top
        tops.append(top)
        totals.append(jnp.sum(weights, axis=0, keepdims=True))
        inners.append(jnp.sum(weights * grad_prob[span], axis=0, keepdims=True))
    best = functools.reduce(jnp.maximum, tops)
    factors = [jnp.exp2((top - best) * EXPO) for top in tops]
    total = sum(factor * part for factor, part in zip(factors, totals))
    inner = sum(factor * part for factor, part in zip(factors, inners))
    return best, total, inner


def grads_tile(key_t, query_tile, grad_tile, log_row, delta_row, weight_ref, prob_ref, top_ref):
    rows = weight_ref.shape[0] // PIECES
    probs, scores = [], []
    for piece in range(PIECES):
        span = slice(piece * rows, piece * rows + rows)
        prob = weight_ref[span] * jnp.exp2((top_ref[piece : piece + 1] - log_row) * EXPO)
        probs.append(prob.astype(jnp.bfloat16))
        scores.append((prob * (prob_ref[span] - delta_row)).astype(jnp.bfloat16))
    prob_half = jnp.concatenate(probs, axis=0)
    grad_score = jnp.concatenate(scores, axis=0)
    grad_key = dot(grad_score, query_tile)
    grad_value = dot(prob_half, grad_tile)
    grad_query = dot(key_t, grad_score).T
    return grad_query, grad_key, grad_value


def quarter_swap(parts, target):
    lane = lax.broadcasted_iota(jnp.int32, parts[0].shape, 1) // QCHUNK
    out = jnp.zeros(parts[0].shape, jnp.float32)
    for source, part in enumerate(parts):
        shift = ((source - target) * QCHUNK) % 128
        moved = pltpu.roll(part, shift, 1) if shift else part
        out = jnp.where(lane == source, moved, out)
    return out


def kernel(n, nh, heads, chunks, *refs):
    refs = list(refs)
    sent_code, own_list = refs[:2]
    refs = refs[2:]
    q_ref, k_ref, v_ref, g_ref = refs[:4]
    dq_ref, dk_ref, dv_ref = refs[4:7]
    g_own, k_t, dk_acc, dv_acc, dq_own = refs[7:12]
    stat_far, stat_own, own_rows, far_rows, logs_own, log_far, delta_far, log_head, delta_head = refs[12:21]
    head_send, head_recv = refs[21:23]
    far_kept, high_kept, low_kept = refs[23:26], refs[26:29], refs[29:32]
    rest = refs[32:]
    buffers = []
    for _ in chunks:
        buffers.append(rest[:20])
        rest = rest[20:]

    me = lax.axis_index("seq")
    hx = lax.axis_index("head")
    stretches = q_ref.shape[0]
    block = stretches * QCHUNK
    feats = heads * HD
    piece = stretches // nh
    tiles = n // TILE_SLOTS
    first_tile = (me + 1) // TILE_SLOTS

    def head_cols(head):
        return pl.ds(pl.multiple_of(head * HD, HD), HD)

    barrier = pltpu.get_barrier_semaphore()

    def greet_seq(step, carry):
        peer = lax.rem(me + step, n)
        pl.semaphore_signal(barrier, inc=1, device_id=(peer, hx), device_id_type=MESH)
        return carry

    def greet_head(step, carry):
        peer = lax.rem(hx + step, nh)
        pl.semaphore_signal(barrier, inc=1, device_id=(me, peer), device_id_type=MESH)
        return carry

    lax.fori_loop(1, n, greet_seq, 0)
    lax.fori_loop(1, nh, greet_head, 0)
    pl.semaphore_wait(barrier, n - 1 + nh - 1)

    def head_copy(peer, slot):
        return pltpu.make_async_remote_copy(
            src_ref=g_ref.at[:, :, pl.ds(pl.multiple_of(peer * feats, HD), feats)],
            dst_ref=g_own.at[pl.ds(slot * piece, piece)],
            send_sem=head_send.at[peer],
            recv_sem=head_recv.at[slot],
            device_id=(me, peer),
            device_id_type=MESH,
        )

    def start_head(step, carry):
        head_copy(lax.rem(hx + step, nh), hx).start()
        return carry

    lax.fori_loop(1, nh, start_head, 0)

    def pair_copy(src, dst, send, recv, peer, slot):
        return pltpu.make_async_remote_copy(
            src_ref=src.at[peer],
            dst_ref=dst.at[slot],
            send_sem=send.at[peer],
            recv_sem=recv.at[slot],
            device_id=(peer, hx),
            device_id_type=MESH,
        )

    def each_near(body):
        def step(i, carry):
            place = me - 1 - i
            hop = place // 2
            body(hop + (place % 2) * (me - 1 - 2 * hop))
            return carry

        lax.fori_loop(0, me, step, 0)

    def each_far(body):
        def step(i, carry):
            place = n - 2 - me - i
            hop = place // 2
            body(n - 1 - hop - (place % 2) * (n - 2 - me - 2 * hop))
            return carry

        lax.fori_loop(0, n - 1 - me, step, 0)

    def start_down(src, dst, send, recv):
        each_near(lambda peer: pair_copy(src, dst, send, recv, peer, me).start())

    def gather_rows(source, kind):
        def body(peer):
            row = jnp.maximum(sent_code[peer] - 1, 0)
            for (start, stop), group in zip(chunks, groups):
                for head in range(start, stop):
                    group[kind][0][peer, head - start] = source[row, :, head * HD : head * HD + HD]
            pair_copy(*groups[0][kind], peer, me).start()

        each_near(body)

    def wait_far(src, dst, send, recv):
        def step(peer, carry):
            pair_copy(src, dst, send, recv, peer, peer).wait_recv()
            return carry

        lax.fori_loop(me + 1, n, step, 0)

    def wait_near(src, dst, send, recv):
        def step(peer, carry):
            pair_copy(src, dst, send, recv, peer, peer).wait_recv()
            return carry

        lax.fori_loop(0, me, step, 0)

    def sent_down(src, dst, send, recv):
        def step(peer, carry):
            pair_copy(src, dst, send, recv, peer, me).wait_send()
            return carry

        lax.fori_loop(0, me, step, 0)

    def start_up(src, dst, send, recv):
        each_far(lambda peer: pair_copy(src, dst, send, recv, peer, me).start())

    def sent_up(src, dst, send, recv):
        def step(peer, carry):
            pair_copy(src, dst, send, recv, peer, me).wait_send()
            return carry

        lax.fori_loop(me + 1, n, step, 0)

    groups = []
    for held in buffers:
        groups.append(tuple(tuple(held[4 * i : 4 * i + 4]) for i in range(5)))

    gather_rows(q_ref, 0)
    start_down(*groups[1][0])

    def clear(slot, carry):
        for rows, grads, stats, logs, parts in groups:
            rows[1][slot] = jnp.zeros(rows[1].shape[1:], jnp.bfloat16)
            grads[1][slot] = jnp.zeros(grads[1].shape[1:], jnp.bfloat16)
            logs[1][slot, 0:1] = jnp.full((1, 128), BIG, jnp.float32)
            logs[1][slot, 1:2] = jnp.zeros((1, 128), jnp.float32)
        return carry

    lax.fori_loop(0, me + 1, clear, 0)

    def turn(head, carry):
        k_t[head] = k_ref[:, head_cols(head)].T
        return carry

    lax.fori_loop(0, heads, turn, 0)

    g_own[pl.ds(hx * piece, piece)] = g_ref[:, :, pl.ds(pl.multiple_of(hx * feats, HD), feats)]

    def wait_head(step, carry):
        peer = lax.rem(hx + step, nh)
        head_copy(peer, peer).wait_recv()
        return carry

    lax.fori_loop(1, nh, wait_head, 0)
    gather_rows(g_own, 1)

    half = block // 2
    middle = stretches // 2

    def own_tile(source, upper, cols):
        places = slice(middle, stretches) if upper else slice(0, middle)
        return source[places, :, cols].reshape(half, HD)

    def pad_stats(top, total, inner):
        return jnp.concatenate([top, total, inner, jnp.zeros((5, top.shape[1]), jnp.float32)], axis=0)

    def own_stats(head, carry):
        cols = head_cols(head)
        stat_own[head, :, 0:half] = pad_stats(
            *stats_tile(
                k_ref[0:half, cols], v_ref[0:half, cols], own_tile(q_ref, False, cols), own_tile(g_own, False, cols), 0,
                *(kept.at[head] for kept in low_kept),
            )
        )
        stat_own[head, :, half:block] = pad_stats(
            *stats_tile(
                k_ref[:, cols], v_ref[:, cols], own_tile(q_ref, True, cols), own_tile(g_own, True, cols), half,
                *(kept.at[head] for kept in high_kept),
            )
        )
        return carry

    lax.fori_loop(0, heads, own_stats, 0)
    for chunk, (start, stop) in enumerate(chunks):
        for group in range(stretches // GROUP):
            held = [stat_own[head, :, group * 128 : group * 128 + 128] for head in range(start, stop)]
            for slot in range(GROUP):
                swapped = quarter_swap(held, slot)
                row = group * GROUP + slot
                for kind in range(3):
                    own_rows[chunk, kind, row : row + 1] = swapped[kind : kind + 1]

    last = len(chunks)
    low_lanes = lax.broadcasted_iota(jnp.int32, (1, 128), 1) < 64

    def chunk_stats(chunk):
        (start, stop), (rows, grads, stats, logs, parts) = chunks[chunk], groups[chunk]
        count = stop - start
        wait_far(*rows)
        wait_far(*grads)

        def far_stats(tile, carry):
            slots = pl.ds(pl.multiple_of(tile * TILE_SLOTS, TILE_SLOTS), TILE_SLOTS)
            for local in range(count):
                cols = pl.ds((local + start) * HD, HD)
                query_tile = rows[1][slots, local].reshape(TILE, HD)
                grad_tile = grads[1][slots, local].reshape(TILE, HD)
                stat_far[local, :, pl.ds(pl.multiple_of(tile * TILE, TILE), TILE)] = pad_stats(
                    *stats_tile(
                        k_ref[:, cols], v_ref[:, cols], query_tile, grad_tile, None,
                        *(kept.at[chunk % 2, local, tile] for kept in far_kept),
                    )
                )
            return carry

        lax.fori_loop(first_tile, tiles, far_stats, 0)

        def far_swap(group, carry):
            lanes = pl.ds(pl.multiple_of(group * 128, 128), 128)
            held = [stat_far[local, :, lanes] for local in range(count)]
            for slot in range(GROUP):
                swapped = quarter_swap(held, slot)
                moved = pltpu.roll(swapped, 64, 1)
                stats[0][group * GROUP + slot, 0:1] = jnp.where(low_lanes, swapped[0:1], moved[1:2])
                stats[0][group * GROUP + slot, 1:2] = swapped[2:3]
            return carry

        lax.fori_loop(first_tile * (TILE // 128), n // GROUP, far_swap, 0)
        start_up(*stats)

    def chunk_logs(chunk):
        (start, stop), (rows, grads, stats, logs, parts) = chunks[chunk], groups[chunk]
        count = stop - start
        wait_near(*stats)
        fill = jnp.where(low_lanes, NEG, 0.0)
        for row in range(stretches):
            for pick in range(3):
                source = own_list[row * 3 + pick]
                live = jnp.full((1, 128), source, jnp.int32) != me
                far_rows[pick, 0, row : row + 1] = jnp.where(live, stats[1][source, 0:1], fill)
                far_rows[pick, 2, row : row + 1] = jnp.where(live, stats[1][source, 1:2], 0.0)
        for pick in range(3):
            far_rows[pick, 1] = pltpu.roll(far_rows[pick, 0], 64, 1)
        best = own_rows[chunk, 0]
        for pick in range(3):
            best = jnp.maximum(best, far_rows[pick, 0])
        weight = jnp.exp2((own_rows[chunk, 0] - best) * EXPO)
        total = own_rows[chunk, 1] * weight
        inner = own_rows[chunk, 2] * weight
        for pick in range(3):
            weight = jnp.exp2((far_rows[pick, 0] - best) * EXPO)
            total += far_rows[pick, 1] * weight
            inner += far_rows[pick, 2] * weight
        log_total = best + (jnp.log(total) - math.log(SCALE)) * (1.0 / SCALE)
        delta = inner / total
        for row in range(stretches):
            logs_own[row, 0:1] = log_total[row : row + 1]
            logs_own[row, 1:2] = delta[row : row + 1]

        for peer in range(n - 1):
            row = jnp.maximum(sent_code[peer] - 1, 0)
            used = jnp.full((1, 128), sent_code[peer], jnp.int32) > 0
            logs[0][peer, 0:1] = jnp.where(used, logs_own[row, 0:1], BIG)
            logs[0][peer, 1:2] = jnp.where(used, logs_own[row, 1:2], 0.0)
        start_down(*logs)

        for group in range(stretches // GROUP):
            for kind, kept in ((0, log_head), (1, delta_head)):
                lines = [
                    jnp.broadcast_to(logs_own[group * GROUP + slot, kind : kind + 1], (8, 128))
                    for slot in range(GROUP)
                ]
                for local in range(count):
                    kept[local, :, group * 128 : group * 128 + 128] = quarter_swap(lines, local)

    def chunk_own(chunk):
        (start, stop), (rows, grads, stats, logs, parts) = chunks[chunk], groups[chunk]
        count = stop - start
        def own_grads(local, carry):
            head = local + start
            cols = head_cols(head)
            grad_query, grad_key, grad_value = grads_tile(
                k_t[head], own_tile(q_ref, True, cols), own_tile(g_own, True, cols),
                log_head[local, 0:1, half:block], delta_head[local, 0:1, half:block],
                *(kept.at[head] for kept in high_kept),
            )
            dq_own[head, half:block] = grad_query
            dk_acc[head] = grad_key
            dv_acc[head] = grad_value
            grad_query, grad_key, grad_value = grads_tile(
                k_t[head, :, 0:half], own_tile(q_ref, False, cols), own_tile(g_own, False, cols),
                log_head[local, 0:1, 0:half], delta_head[local, 0:1, 0:half],
                *(kept.at[head] for kept in low_kept),
            )
            dq_own[head, 0:half] = grad_query
            dk_acc[head, 0:half] += grad_key
            dv_acc[head, 0:half] += grad_value
            return carry

        lax.fori_loop(0, count, own_grads, 0)

    def chunk_far(chunk):
        (start, stop), (rows, grads, stats, logs, parts) = chunks[chunk], groups[chunk]
        count = stop - start
        wait_far(*logs)

        def far_logs(group, carry):
            lanes = pl.ds(pl.multiple_of(group * 128, 128), 128)
            for kind, kept in ((0, log_far), (1, delta_far)):
                lines = [
                    jnp.broadcast_to(logs[1][group * GROUP + slot, kind : kind + 1], (8, 128)) for slot in range(GROUP)
                ]
                for local in range(count):
                    kept[local, :, lanes] = quarter_swap(lines, local)
            return carry

        lax.fori_loop(first_tile * (TILE // 128), n // GROUP, far_logs, 0)

        def far_grads(tile, carry):
            slots = pl.ds(pl.multiple_of(tile * TILE_SLOTS, TILE_SLOTS), TILE_SLOTS)
            lanes = pl.ds(pl.multiple_of(tile * TILE, TILE), TILE)
            for local in range(count):
                head = local + start
                query_tile = rows[1][slots, local].reshape(TILE, HD)
                grad_tile = grads[1][slots, local].reshape(TILE, HD)
                grad_query, grad_key, grad_value = grads_tile(
                    k_t[head], query_tile, grad_tile, log_far[local, 0:1, lanes], delta_far[local, 0:1, lanes],
                    *(kept.at[chunk % 2, local, tile] for kept in far_kept),
                )
                parts[0][slots, local] = grad_query.astype(jnp.bfloat16).reshape(TILE_SLOTS, QCHUNK, HD)
                dk_acc[head] += grad_key
                dv_acc[head] += grad_value
            return carry

        lax.fori_loop(first_tile, tiles, far_grads, 0)

    for chunk in range(last):
        chunk_stats(chunk)
        if chunk + 1 < last:
            start_down(*groups[chunk + 1][1])
        if chunk > 0:
            chunk_far(chunk - 1)
        chunk_logs(chunk)
        if chunk + 2 < last:
            start_down(*groups[chunk + 2][0])
        if chunk > 0:
            start_up(*groups[chunk - 1][4])
        chunk_own(chunk)

    def all_sent():
        def head_sent(step, carry):
            head_copy(lax.rem(hx + step, nh), hx).wait_send()
            return carry

        lax.fori_loop(1, nh, head_sent, 0)
        for rows, grads, stats, logs, parts in groups:
            sent_down(*rows)
            sent_down(*grads)
            sent_up(*stats)
            sent_down(*logs)
            sent_up(*parts)

    def chunk_queries(chunk):
        (start, stop), parts = chunks[chunk], groups[chunk][4]
        wait_near(*parts)

        def write_queries(row, carry):
            place = pl.ds(pl.multiple_of(row * QCHUNK, QCHUNK), QCHUNK)
            for local in range(stop - start):
                total = dq_own[start + local, place]
                for pick in range(3):
                    source = own_list[row * 3 + pick]
                    live = jnp.full((QCHUNK, HD), source, jnp.int32) != me
                    far = parts[1][source, local].astype(jnp.float32)
                    total += jnp.where(live, far, 0.0)
                dq_ref[place, pl.ds((start + local) * HD, HD)] = total.astype(jnp.bfloat16)
            return carry

        lax.fori_loop(0, stretches, write_queries, 0)

    def write_keys(head, carry):
        cols = head_cols(head)
        dk_ref[:, cols] = dk_acc[head].astype(jnp.bfloat16)
        dv_ref[:, cols] = (dv_acc[head] * math.sqrt(HD)).astype(jnp.bfloat16)
        return carry

    for chunk in range(last - 2):
        chunk_queries(chunk)
    chunk_far(last - 1)
    start_up(*groups[last - 1][4])
    lax.fori_loop(0, heads, write_keys, 0)
    chunk_queries(last - 2)
    all_sent()
    chunk_queries(last - 1)


def attention_grads(n, nh, tables, queries, keys, values, out_grad):
    block, feats = queries.shape
    heads = feats // HD
    chunks = head_chunks(heads)
    stretches = block // QCHUNK
    bf, f32 = jnp.bfloat16, jnp.float32
    dma = pltpu.SemaphoreType.DMA
    most = max(stop - start for start, stop in chunks)
    scratch = [
        pltpu.VMEM((stretches, QCHUNK, feats), bf),
        pltpu.VMEM((heads, HD, block), bf),
        pltpu.VMEM((heads, block, HD), f32),
        pltpu.VMEM((heads, block, HD), f32),
        pltpu.VMEM((heads, block, HD), f32),
        pltpu.VMEM((most, 8, n * QCHUNK), f32),
        pltpu.VMEM((heads, 8, block), f32),
        pltpu.VMEM((len(chunks), 3, stretches, 128), f32),
        pltpu.VMEM((3, 3, stretches, 128), f32),
        pltpu.VMEM((stretches, 2, 128), f32),
        pltpu.VMEM((most, 8, n * QCHUNK), f32),
        pltpu.VMEM((most, 8, n * QCHUNK), f32),
        pltpu.VMEM((most, 8, block), f32),
        pltpu.VMEM((most, 8, block), f32),
        dma((nh,)),
        dma((nh,)),
    ]
    half = block // 2
    for lead, keys_held, cols_held in (
        ((2, most, n // TILE_SLOTS), block, TILE),
        ((heads,), block, half),
        ((heads,), half, half),
    ):
        scratch += [pltpu.VMEM((*lead, rows, cols_held), f32) for rows in (keys_held, keys_held, 8)]
    for start, stop in chunks:
        row_shape = (n, stop - start, QCHUNK, HD)
        for shape, dtype in (
            (row_shape, bf),
            (row_shape, bf),
            ((n, 2, 128), f32),
            ((n, 2, 128), f32),
            (row_shape, bf),
        ):
            scratch += [pltpu.VMEM(shape, dtype), pltpu.VMEM(shape, dtype), dma((n,)), dma((n,))]
    whole = pl.BlockSpec(memory_space=pltpu.VMEM)
    small = pl.BlockSpec(memory_space=pltpu.SMEM)
    out = jax.ShapeDtypeStruct((block, feats), bf)
    pairs = (n + stretches) // 2 * QCHUNK * block * feats
    return pl.pallas_call(
        functools.partial(kernel, n, nh, heads, chunks),
        out_shape=(out, out, out),
        in_specs=[small] * 2 + [whole] * 4,
        out_specs=(whole, whole, whole),
        scratch_shapes=scratch,
        cost_estimate=pl.CostEstimate(flops=14 * pairs, bytes_accessed=14 * block * feats, transcendentals=0),
        compiler_params=pltpu.CompilerParams(
            collective_id=0, has_side_effects=True, vmem_limit_bytes=60 * 1024 * 1024
        ),
    )(*tables, queries.reshape(stretches, QCHUNK, feats), keys, values, out_grad.reshape(-1, QCHUNK, nh * feats))


def per_device(queries, keys, values, out_grad, selection):
    n = lax.axis_size("seq")
    nh = lax.axis_size("head")
    me = lax.axis_index("seq")
    stretches = queries.shape[0] // QCHUNK
    own = lax.dynamic_slice_in_dim(selection, me * stretches, stretches, 0)
    hits = (own[:, :, None] == jnp.arange(n, dtype=jnp.int32)) & (own != me)[:, :, None]
    places = jnp.arange(1, stretches + 1, dtype=jnp.int32)[:, None, None]
    tables = (jnp.sum(jnp.where(hits, places, 0), axis=(0, 1)), own.reshape(-1))
    return attention_grads(n, nh, tables, queries, keys, values, out_grad)


def solution(mesh):
    return jax.shard_map(
        per_device,
        mesh=mesh,
        in_specs=(
            P("seq", "head"),
            P("seq", "head"),
            P("seq", "head"),
            P(("seq", "head"), None),
            P(),
        ),
        out_specs=(P("seq", "head"), P("seq", "head"), P("seq", "head")),
        check_vma=False,
    )
```

```python
import functools
import math

import jax
import jax.numpy as jnp
from jax import lax
from jax.experimental import pallas as pl
from jax.experimental.pallas import tpu as pltpu
from jax.sharding import PartitionSpec as P

HD = 128
QCHUNK = 32
TILE_SLOTS = 8
TILE = TILE_SLOTS * QCHUNK
GROUP = 128 // QCHUNK
PIECES = 4
SCALE = 1.0 / math.sqrt(HD)
EXPO = SCALE * math.log2(math.e)
NEG = -1e30
BIG = 1e30
NT_DIMS = (((1,), (1,)), ((), ()))
MESH = pl.DeviceIdType.MESH


def head_chunks(head_count):
    edges = list(range(0, head_count, 2)) + [head_count]
    return tuple(zip(edges[:-1], edges[1:]))


def dot(lhs, rhs):
    return jnp.dot(lhs, rhs, preferred_element_type=jnp.float32)


def dot_nt(lhs, rhs):
    return lax.dot_general(lhs, rhs, NT_DIMS, preferred_element_type=jnp.float32)


def score_columns(key_tile, query_tile, diagonal):
    scores = dot_nt(key_tile, query_tile)
    if diagonal is not None:
        rows = lax.broadcasted_iota(jnp.int32, scores.shape, 0)
        cols = lax.broadcasted_iota(jnp.int32, scores.shape, 1)
        scores = jnp.where(rows <= cols + diagonal, scores, NEG)
    return scores


def stats_tile(key_tile, value_tile, query_tile, grad_tile, diagonal, weight_ref, prob_ref, top_ref):
    scores = score_columns(key_tile, query_tile, diagonal)
    grad_prob = dot_nt(value_tile, grad_tile)
    prob_ref[...] = grad_prob
    rows = scores.shape[0] // PIECES
    tops, totals, inners = [], [], []
    for piece in range(PIECES):
        span = slice(piece * rows, piece * rows + rows)
        top = jnp.max(scores[span], axis=0, keepdims=True)
        weights = jnp.exp2((scores[span] - top) * EXPO)
        weight_ref[span] = weights
        top_ref[piece : piece + 1] = top
        tops.append(top)
        totals.append(jnp.sum(weights, axis=0, keepdims=True))
        inners.append(jnp.sum(weights * grad_prob[span], axis=0, keepdims=True))
    best = functools.reduce(jnp.maximum, tops)
    factors = [jnp.exp2((top - best) * EXPO) for top in tops]
    total = sum(factor * part for factor, part in zip(factors, totals))
    inner = sum(factor * part for factor, part in zip(factors, inners))
    return best, total, inner


def grads_tile(key_t, query_tile, grad_tile, log_row, delta_row, weight_ref, prob_ref, top_ref):
    rows = weight_ref.shape[0] // PIECES
    probs, scores = [], []
    for piece in range(PIECES):
        span = slice(piece * rows, piece * rows + rows)
        prob = weight_ref[span] * jnp.exp2((top_ref[piece : piece + 1] - log_row) * EXPO)
        probs.append(prob.astype(jnp.bfloat16))
        scores.append((prob * (prob_ref[span] - delta_row)).astype(jnp.bfloat16))
    prob_half = jnp.concatenate(probs, axis=0)
    grad_score = jnp.concatenate(scores, axis=0)
    grad_key = dot(grad_score, query_tile)
    grad_value = dot(prob_half, grad_tile)
    grad_query = dot(key_t, grad_score).T
    return grad_query, grad_key, grad_value


def quarter_swap(parts, target):
    lane = lax.broadcasted_iota(jnp.int32, parts[0].shape, 1) // QCHUNK
    out = jnp.zeros(parts[0].shape, jnp.float32)
    for source, part in enumerate(parts):
        shift = ((source - target) * QCHUNK) % 128
        moved = pltpu.roll(part, shift, 1) if shift else part
        out = jnp.where(lane == source, moved, out)
    return out


def kernel(n, nh, heads, chunks, *refs):
    refs = list(refs)
    sent_code, own_list = refs[:2]
    refs = refs[2:]
    q_ref, k_ref, v_ref, g_ref = refs[:4]
    dq_ref, dk_ref, dv_ref = refs[4:7]
    g_own, k_t, dk_acc, dv_acc, dq_own = refs[7:12]
    stat_far, stat_own, own_rows, far_rows, logs_own, log_far, delta_far, log_head, delta_head = refs[12:21]
    head_send, head_recv = refs[21:23]
    far_kept, high_kept, low_kept = refs[23:26], refs[26:29], refs[29:32]
    rest = refs[32:]
    buffers = []
    for _ in chunks:
        buffers.append(rest[:20])
        rest = rest[20:]

    me = lax.axis_index("seq")
    hx = lax.axis_index("head")
    stretches = q_ref.shape[0]
    block = stretches * QCHUNK
    feats = heads * HD
    piece = stretches // nh
    tiles = n // TILE_SLOTS
    first_tile = (me + 1) // TILE_SLOTS

    def head_cols(head):
        return pl.ds(pl.multiple_of(head * HD, HD), HD)

    barrier = pltpu.get_barrier_semaphore()

    def greet_seq(step, carry):
        peer = lax.rem(me + step, n)
        pl.semaphore_signal(barrier, inc=1, device_id=(peer, hx), device_id_type=MESH)
        return carry

    def greet_head(step, carry):
        peer = lax.rem(hx + step, nh)
        pl.semaphore_signal(barrier, inc=1, device_id=(me, peer), device_id_type=MESH)
        return carry

    lax.fori_loop(1, n, greet_seq, 0)
    lax.fori_loop(1, nh, greet_head, 0)
    pl.semaphore_wait(barrier, n - 1 + nh - 1)

    def head_copy(peer, slot):
        return pltpu.make_async_remote_copy(
            src_ref=g_ref.at[:, :, pl.ds(pl.multiple_of(peer * feats, HD), feats)],
            dst_ref=g_own.at[pl.ds(slot * piece, piece)],
            send_sem=head_send.at[peer],
            recv_sem=head_recv.at[slot],
            device_id=(me, peer),
            device_id_type=MESH,
        )

    def start_head(step, carry):
        head_copy(lax.rem(hx + step, nh), hx).start()
        return carry

    lax.fori_loop(1, nh, start_head, 0)

    def pair_copy(src, dst, send, recv, peer, slot):
        return pltpu.make_async_remote_copy(
            src_ref=src.at[peer],
            dst_ref=dst.at[slot],
            send_sem=send.at[peer],
            recv_sem=recv.at[slot],
            device_id=(peer, hx),
            device_id_type=MESH,
        )

    def each_near(body):
        def step(i, carry):
            place = me - 1 - i
            hop = place // 2
            body(hop + (place % 2) * (me - 1 - 2 * hop))
            return carry

        lax.fori_loop(0, me, step, 0)

    def each_far(body):
        def step(i, carry):
            place = n - 2 - me - i
            hop = place // 2
            body(n - 1 - hop - (place % 2) * (n - 2 - me - 2 * hop))
            return carry

        lax.fori_loop(0, n - 1 - me, step, 0)

    def start_down(src, dst, send, recv):
        each_near(lambda peer: pair_copy(src, dst, send, recv, peer, me).start())

    def gather_rows(source, kind):
        def body(peer):
            row = jnp.maximum(sent_code[peer] - 1, 0)
            for (start, stop), group in zip(chunks, groups):
                for head in range(start, stop):
                    group[kind][0][peer, head - start] = source[row, :, head * HD : head * HD + HD]
            pair_copy(*groups[0][kind], peer, me).start()

        each_near(body)

    def wait_far(src, dst, send, recv):
        def step(peer, carry):
            pair_copy(src, dst, send, recv, peer, peer).wait_recv()
            return carry

        lax.fori_loop(me + 1, n, step, 0)

    def wait_near(src, dst, send, recv):
        def step(peer, carry):
            pair_copy(src, dst, send, recv, peer, peer).wait_recv()
            return carry

        lax.fori_loop(0, me, step, 0)

    def sent_down(src, dst, send, recv):
        def step(peer, carry):
            pair_copy(src, dst, send, recv, peer, me).wait_send()
            return carry

        lax.fori_loop(0, me, step, 0)

    def start_up(src, dst, send, recv):
        each_far(lambda peer: pair_copy(src, dst, send, recv, peer, me).start())

    def sent_up(src, dst, send, recv):
        def step(peer, carry):
            pair_copy(src, dst, send, recv, peer, me).wait_send()
            return carry

        lax.fori_loop(me + 1, n, step, 0)

    groups = []
    for held in buffers:
        groups.append(tuple(tuple(held[4 * i : 4 * i + 4]) for i in range(5)))

    gather_rows(q_ref, 0)
    start_down(*groups[1][0])

    def clear(slot, carry):
        for rows, grads, stats, logs, parts in groups:
            rows[1][slot] = jnp.zeros(rows[1].shape[1:], jnp.bfloat16)
            grads[1][slot] = jnp.zeros(grads[1].shape[1:], jnp.bfloat16)
            logs[1][slot, 0:1] = jnp.full((1, 128), BIG, jnp.float32)
            logs[1][slot, 1:2] = jnp.zeros((1, 128), jnp.float32)
        return carry

    lax.fori_loop(0, me + 1, clear, 0)

    def turn(head, carry):
        k_t[head] = k_ref[:, head_cols(head)].T
        return carry

    lax.fori_loop(0, heads, turn, 0)

    g_own[pl.ds(hx * piece, piece)] = g_ref[:, :, pl.ds(pl.multiple_of(hx * feats, HD), feats)]

    def wait_head(step, carry):
        peer = lax.rem(hx + step, nh)
        head_copy(peer, peer).wait_recv()
        return carry

    lax.fori_loop(1, nh, wait_head, 0)
    gather_rows(g_own, 1)
    start_down(*groups[1][1])

    half = block // 2
    middle = stretches // 2

    def own_tile(source, upper, cols):
        places = slice(middle, stretches) if upper else slice(0, middle)
        return source[places, :, cols].reshape(half, HD)

    def pad_stats(top, total, inner):
        return jnp.concatenate([top, total, inner, jnp.zeros((5, top.shape[1]), jnp.float32)], axis=0)

    def own_stats(head, carry):
        cols = head_cols(head)
        stat_own[head, :, 0:half] = pad_stats(
            *stats_tile(
                k_ref[0:half, cols], v_ref[0:half, cols], own_tile(q_ref, False, cols), own_tile(g_own, False, cols), 0,
                *(kept.at[head] for kept in low_kept),
            )
        )
        stat_own[head, :, half:block] = pad_stats(
            *stats_tile(
                k_ref[:, cols], v_ref[:, cols], own_tile(q_ref, True, cols), own_tile(g_own, True, cols), half,
                *(kept.at[head] for kept in high_kept),
            )
        )
        return carry

    lax.fori_loop(0, heads, own_stats, 0)
    for chunk, (start, stop) in enumerate(chunks):
        for group in range(stretches // GROUP):
            held = [stat_own[head, :, group * 128 : group * 128 + 128] for head in range(start, stop)]
            for slot in range(GROUP):
                swapped = quarter_swap(held, slot)
                row = group * GROUP + slot
                for kind in range(3):
                    own_rows[chunk, kind, row : row + 1] = swapped[kind : kind + 1]

    last = len(chunks)
    low_lanes = lax.broadcasted_iota(jnp.int32, (1, 128), 1) < 64

    def chunk_stats(chunk):
        (start, stop), (rows, grads, stats, logs, parts) = chunks[chunk], groups[chunk]
        count = stop - start
        wait_far(*rows)
        wait_far(*grads)

        def far_stats(tile, carry):
            slots = pl.ds(pl.multiple_of(tile * TILE_SLOTS, TILE_SLOTS), TILE_SLOTS)
            for local in range(count):
                cols = pl.ds((local + start) * HD, HD)
                query_tile = rows[1][slots, local].reshape(TILE, HD)
                grad_tile = grads[1][slots, local].reshape(TILE, HD)
                stat_far[local, :, pl.ds(pl.multiple_of(tile * TILE, TILE), TILE)] = pad_stats(
                    *stats_tile(
                        k_ref[:, cols], v_ref[:, cols], query_tile, grad_tile, None,
                        *(kept.at[chunk % 2, local, tile] for kept in far_kept),
                    )
                )
            return carry

        lax.fori_loop(first_tile, tiles, far_stats, 0)

        def far_swap(group, carry):
            lanes = pl.ds(pl.multiple_of(group * 128, 128), 128)
            held = [stat_far[local, :, lanes] for local in range(count)]
            for slot in range(GROUP):
                swapped = quarter_swap(held, slot)
                moved = pltpu.roll(swapped, 64, 1)
                stats[0][group * GROUP + slot, 0:1] = jnp.where(low_lanes, swapped[0:1], moved[1:2])
                stats[0][group * GROUP + slot, 1:2] = swapped[2:3]
            return carry

        lax.fori_loop(first_tile * (TILE // 128), n // GROUP, far_swap, 0)
        start_up(*stats)

    def chunk_logs(chunk):
        (start, stop), (rows, grads, stats, logs, parts) = chunks[chunk], groups[chunk]
        count = stop - start
        wait_near(*stats)
        fill = jnp.where(low_lanes, NEG, 0.0)
        for row in range(stretches):
            for pick in range(3):
                source = own_list[row * 3 + pick]
                live = jnp.full((1, 128), source, jnp.int32) != me
                far_rows[pick, 0, row : row + 1] = jnp.where(live, stats[1][source, 0:1], fill)
                far_rows[pick, 2, row : row + 1] = jnp.where(live, stats[1][source, 1:2], 0.0)
        for pick in range(3):
            far_rows[pick, 1] = pltpu.roll(far_rows[pick, 0], 64, 1)
        best = own_rows[chunk, 0]
        for pick in range(3):
            best = jnp.maximum(best, far_rows[pick, 0])
        weight = jnp.exp2((own_rows[chunk, 0] - best) * EXPO)
        total = own_rows[chunk, 1] * weight
        inner = own_rows[chunk, 2] * weight
        for pick in range(3):
            weight = jnp.exp2((far_rows[pick, 0] - best) * EXPO)
            total += far_rows[pick, 1] * weight
            inner += far_rows[pick, 2] * weight
        log_total = best + (jnp.log(total) - math.log(SCALE)) * (1.0 / SCALE)
        delta = inner / total
        for row in range(stretches):
            logs_own[row, 0:1] = log_total[row : row + 1]
            logs_own[row, 1:2] = delta[row : row + 1]

        for peer in range(n - 1):
            row = jnp.maximum(sent_code[peer] - 1, 0)
            used = jnp.full((1, 128), sent_code[peer], jnp.int32) > 0
            logs[0][peer, 0:1] = jnp.where(used, logs_own[row, 0:1], BIG)
            logs[0][peer, 1:2] = jnp.where(used, logs_own[row, 1:2], 0.0)
        start_down(*logs)

        for group in range(stretches // GROUP):
            for kind, kept in ((0, log_head), (1, delta_head)):
                lines = [
                    jnp.broadcast_to(logs_own[group * GROUP + slot, kind : kind + 1], (8, 128))
                    for slot in range(GROUP)
                ]
                for local in range(count):
                    kept[local, :, group * 128 : group * 128 + 128] = quarter_swap(lines, local)

    def chunk_own(chunk):
        (start, stop), (rows, grads, stats, logs, parts) = chunks[chunk], groups[chunk]
        count = stop - start
        def own_grads(local, carry):
            head = local + start
            cols = head_cols(head)
            grad_query, grad_key, grad_value = grads_tile(
                k_t[head], own_tile(q_ref, True, cols), own_tile(g_own, True, cols),
                log_head[local, 0:1, half:block], delta_head[local, 0:1, half:block],
                *(kept.at[head] for kept in high_kept),
            )
            dq_own[head, half:block] = grad_query
            dk_acc[head] = grad_key
            dv_acc[head] = grad_value
            grad_query, grad_key, grad_value = grads_tile(
                k_t[head, :, 0:half], own_tile(q_ref, False, cols), own_tile(g_own, False, cols),
                log_head[local, 0:1, 0:half], delta_head[local, 0:1, 0:half],
                *(kept.at[head] for kept in low_kept),
            )
            dq_own[head, 0:half] = grad_query
            dk_acc[head, 0:half] += grad_key
            dv_acc[head, 0:half] += grad_value
            return carry

        lax.fori_loop(0, count, own_grads, 0)

    def chunk_far(chunk):
        (start, stop), (rows, grads, stats, logs, parts) = chunks[chunk], groups[chunk]
        count = stop - start
        wait_far(*logs)

        def far_logs(group, carry):
            lanes = pl.ds(pl.multiple_of(group * 128, 128), 128)
            for kind, kept in ((0, log_far), (1, delta_far)):
                lines = [
                    jnp.broadcast_to(logs[1][group * GROUP + slot, kind : kind + 1], (8, 128)) for slot in range(GROUP)
                ]
                for local in range(count):
                    kept[local, :, lanes] = quarter_swap(lines, local)
            return carry

        lax.fori_loop(first_tile * (TILE // 128), n // GROUP, far_logs, 0)

        def far_grads(tile, carry):
            slots = pl.ds(pl.multiple_of(tile * TILE_SLOTS, TILE_SLOTS), TILE_SLOTS)
            lanes = pl.ds(pl.multiple_of(tile * TILE, TILE), TILE)
            for local in range(count):
                head = local + start
                query_tile = rows[1][slots, local].reshape(TILE, HD)
                grad_tile = grads[1][slots, local].reshape(TILE, HD)
                grad_query, grad_key, grad_value = grads_tile(
                    k_t[head], query_tile, grad_tile, log_far[local, 0:1, lanes], delta_far[local, 0:1, lanes],
                    *(kept.at[chunk % 2, local, tile] for kept in far_kept),
                )
                parts[0][slots, local] = grad_query.astype(jnp.bfloat16).reshape(TILE_SLOTS, QCHUNK, HD)
                dk_acc[head] += grad_key
                dv_acc[head] += grad_value
            return carry

        lax.fori_loop(first_tile, tiles, far_grads, 0)

    for chunk in range(last):
        chunk_stats(chunk)
        if chunk > 1:
            start_up(*groups[chunk - 2][4])
        if chunk + 2 < last:
            start_down(*groups[chunk + 2][0])
        if chunk > 0:
            chunk_far(chunk - 1)
        chunk_logs(chunk)
        if chunk + 2 < last:
            start_down(*groups[chunk + 2][1])
        if chunk == last - 1:
            start_up(*groups[chunk - 1][4])
        chunk_own(chunk)

    def all_sent():
        def head_sent(step, carry):
            head_copy(lax.rem(hx + step, nh), hx).wait_send()
            return carry

        lax.fori_loop(1, nh, head_sent, 0)
        for rows, grads, stats, logs, parts in groups:
            sent_down(*rows)
            sent_down(*grads)
            sent_up(*stats)
            sent_down(*logs)
            sent_up(*parts)

    def chunk_queries(chunk):
        (start, stop), parts = chunks[chunk], groups[chunk][4]
        wait_near(*parts)

        def write_queries(row, carry):
            place = pl.ds(pl.multiple_of(row * QCHUNK, QCHUNK), QCHUNK)
            for local in range(stop - start):
                total = dq_own[start + local, place]
                for pick in range(3):
                    source = own_list[row * 3 + pick]
                    live = jnp.full((QCHUNK, HD), source, jnp.int32) != me
                    far = parts[1][source, local].astype(jnp.float32)
                    total += jnp.where(live, far, 0.0)
                dq_ref[place, pl.ds((start + local) * HD, HD)] = total.astype(jnp.bfloat16)
            return carry

        lax.fori_loop(0, stretches, write_queries, 0)

    def write_keys(head, carry):
        cols = head_cols(head)
        dk_ref[:, cols] = dk_acc[head].astype(jnp.bfloat16)
        dv_ref[:, cols] = (dv_acc[head] * math.sqrt(HD)).astype(jnp.bfloat16)
        return carry

    for chunk in range(last - 2):
        chunk_queries(chunk)
    chunk_far(last - 1)
    start_up(*groups[last - 1][4])
    lax.fori_loop(0, heads, write_keys, 0)
    chunk_queries(last - 2)
    all_sent()
    chunk_queries(last - 1)


def attention_grads(n, nh, tables, queries, keys, values, out_grad):
    block, feats = queries.shape
    heads = feats // HD
    chunks = head_chunks(heads)
    stretches = block // QCHUNK
    bf, f32 = jnp.bfloat16, jnp.float32
    dma = pltpu.SemaphoreType.DMA
    most = max(stop - start for start, stop in chunks)
    scratch = [
        pltpu.VMEM((stretches, QCHUNK, feats), bf),
        pltpu.VMEM((heads, HD, block), bf),
        pltpu.VMEM((heads, block, HD), f32),
        pltpu.VMEM((heads, block, HD), f32),
        pltpu.VMEM((heads, block, HD), f32),
        pltpu.VMEM((most, 8, n * QCHUNK), f32),
        pltpu.VMEM((heads, 8, block), f32),
        pltpu.VMEM((len(chunks), 3, stretches, 128), f32),
        pltpu.VMEM((3, 3, stretches, 128), f32),
        pltpu.VMEM((stretches, 2, 128), f32),
        pltpu.VMEM((most, 8, n * QCHUNK), f32),
        pltpu.VMEM((most, 8, n * QCHUNK), f32),
        pltpu.VMEM((most, 8, block), f32),
        pltpu.VMEM((most, 8, block), f32),
        dma((nh,)),
        dma((nh,)),
    ]
    half = block // 2
    for lead, keys_held, cols_held in (
        ((2, most, n // TILE_SLOTS), block, TILE),
        ((heads,), block, half),
        ((heads,), half, half),
    ):
        scratch += [pltpu.VMEM((*lead, rows, cols_held), f32) for rows in (keys_held, keys_held, 8)]
    for start, stop in chunks:
        row_shape = (n, stop - start, QCHUNK, HD)
        for shape, dtype in (
            (row_shape, bf),
            (row_shape, bf),
            ((n, 2, 128), f32),
            ((n, 2, 128), f32),
            (row_shape, bf),
        ):
            scratch += [pltpu.VMEM(shape, dtype), pltpu.VMEM(shape, dtype), dma((n,)), dma((n,))]
    whole = pl.BlockSpec(memory_space=pltpu.VMEM)
    small = pl.BlockSpec(memory_space=pltpu.SMEM)
    out = jax.ShapeDtypeStruct((block, feats), bf)
    pairs = (n + stretches) // 2 * QCHUNK * block * feats
    return pl.pallas_call(
        functools.partial(kernel, n, nh, heads, chunks),
        out_shape=(out, out, out),
        in_specs=[small] * 2 + [whole] * 4,
        out_specs=(whole, whole, whole),
        scratch_shapes=scratch,
        cost_estimate=pl.CostEstimate(flops=14 * pairs, bytes_accessed=14 * block * feats, transcendentals=0),
        compiler_params=pltpu.CompilerParams(
            collective_id=0, has_side_effects=True, vmem_limit_bytes=60 * 1024 * 1024
        ),
    )(*tables, queries.reshape(stretches, QCHUNK, feats), keys, values, out_grad.reshape(-1, QCHUNK, nh * feats))


def per_device(queries, keys, values, out_grad, selection):
    n = lax.axis_size("seq")
    nh = lax.axis_size("head")
    me = lax.axis_index("seq")
    stretches = queries.shape[0] // QCHUNK
    own = lax.dynamic_slice_in_dim(selection, me * stretches, stretches, 0)
    hits = (own[:, :, None] == jnp.arange(n, dtype=jnp.int32)) & (own != me)[:, :, None]
    places = jnp.arange(1, stretches + 1, dtype=jnp.int32)[:, None, None]
    tables = (jnp.sum(jnp.where(hits, places, 0), axis=(0, 1)), own.reshape(-1))
    return attention_grads(n, nh, tables, queries, keys, values, out_grad)


def solution(mesh):
    return jax.shard_map(
        per_device,
        mesh=mesh,
        in_specs=(
            P("seq", "head"),
            P("seq", "head"),
            P("seq", "head"),
            P(("seq", "head"), None),
            P(),
        ),
        out_specs=(P("seq", "head"), P("seq", "head"), P("seq", "head")),
        check_vma=False,
    )
```
